256 devices in a mesh: stn: 32 (over z, x_hi, core), chan: 8 (over y, x_lo).
Axes of the slice: x: 4 (x_hi: 2, x_lo: 2; x = x_hi * 2 + x_lo), y: 4, z: 8, core: 2. Of those that a mesh axis runs over, the one named last changes fastest.
Arguments:
- screen: float32 [64, 512, 512], P('stn'), may hold values from -6 to 6
- pierce_coords: float32 [2, 32, 8, 32, 128], P(None, 'stn', 'chan'), may hold values from 0 to 1
- query_dest: int32 [32, 8, 32, 128], P('stn', 'chan'), may hold values from 0 to 1024, as said below
- positions: float32 [3, 512], P(None, 'stn'), may hold values from -50 to 50
- directions: float32 [3, 512], replicated, may hold values from -0.7 to 0.7
- freq_ratio: float32 [256], P('chan'), may hold values from 0.7 to 1.4
- source_flux: float32 [512], replicated, may hold values from 0.2 to 5
- spectral_index: float32 [512], replicated, may hold values from -1.5 to 0.5
Outputs:
- visibilities: float32 [256, 2, 512, 512], P('chan', None, 'stn')
The draws below stay inside these ranges and needn't reach their ends.
Inputs may be any that keep to these rules, and one draw needn't show every extreme that they name: `query_dest`: in each block every number 0 to 1023 appears in exactly one slot and empty slots hold 1024; an owner's live slots come first in its row; one owner, the same for every block, has all 128 of its slots live in every block.
All inputs are finite; a program needn't handle non-finite values.
Results may differ from the reference program's by a relative error of at most 0.008.
Values may be sent and summed in bfloat16 or wider, within the bound.
A program may use at most 128 MiB of HBM per device.

```python
import math
import jax
import jax.numpy as jnp
from jax import lax

STN_DEV = 16
SRC = 512
TILE = 512
TILES_DEV = 2
STATIONS = 512
CHANNELS = 256
TILES = 64
SRCC = 64
QUERIES = 1024
CAP = 128
N_STN = 32
N_CHAN = 8


def draw_screen(key, part):
    rough = jax.random.normal(jax.random.fold_in(key, 3), (TILES, TILE, TILE), jnp.float32)
    field = 1.5 * rough
    return jnp.clip(field, -6.0, 6.0)


def draw_query_dest(key, part):
    key_order, key_share, key_rank, key_query = jax.random.split(jax.random.fold_in(key, 7), 4)
    blocks = N_STN * N_CHAN
    hot_order = jax.random.permutation(key_order, N_STN).astype(jnp.int32)
    shares = jax.random.randint(key_share, (blocks, N_STN - 1), 1, 4).astype(jnp.int32)
    remain = QUERIES - CAP
    counts = remain * shares // jnp.sum(shares, axis=1, keepdims=True)
    leftover = remain - jnp.sum(counts, axis=1, keepdims=True)
    ranks = jnp.arange(N_STN - 1, dtype=jnp.int32)[None, :]
    counts = counts + (ranks < leftover).astype(jnp.int32)
    counts = jnp.concatenate([jnp.full((blocks, 1), CAP, jnp.int32), counts], axis=1)
    others = jax.vmap(lambda single: jax.random.permutation(single, N_STN - 1))(jax.random.split(key_rank, blocks))
    rank_slot = jnp.concatenate([jnp.zeros((blocks, 1), jnp.int32), others.astype(jnp.int32) + 1], axis=1)
    owner_of = hot_order[rank_slot]
    matches = (owner_of[:, :, None] == jnp.arange(N_STN, dtype=jnp.int32)[None, None, :]).astype(jnp.int32)
    per_owner = jnp.sum(counts[:, :, None] * matches, axis=1)
    starts = jnp.cumsum(per_owner, axis=1) - per_owner
    ordering = jax.vmap(lambda single: jax.random.permutation(single, QUERIES))(jax.random.split(key_query, blocks))
    padded = jnp.concatenate([ordering.astype(jnp.int32), jnp.full((blocks, 1), QUERIES, jnp.int32)], axis=1)
    slots = jnp.arange(CAP, dtype=jnp.int32)[None, None, :]
    live = slots < per_owner[:, :, None]
    positions_in = jnp.where(live, starts[:, :, None] + slots, QUERIES)
    picked = padded[jnp.arange(blocks, dtype=jnp.int32)[:, None, None], positions_in]
    return picked.reshape(N_STN, N_CHAN, N_STN, CAP)


def shard_levels(key, dims, pieces, smallest, high):
    def one(dim, blocks):
        draws = jax.random.uniform(jax.random.fold_in(jax.random.fold_in(key, 6), dim), (blocks,), jnp.float32, smallest / len(pieces), high / len(pieces))
        return jnp.repeat(jnp.exp(draws), dims[dim] // blocks).reshape((-1,) + (1,) * (len(dims) - dim - 1))

    level = one(*pieces[0])
    for cut in pieces[1:]:
        level = level * one(*cut)
    return level


def setup_inputs(seed: int = 0) -> dict:
    splits = jax.random.split(jax.random.key(seed), 9)
    return {
        "screen": draw_screen(jax.random.fold_in(splits[8], 71), 0),
        "pierce_coords": jnp.clip(1.0 * jax.random.uniform(splits[1], (2, N_STN, N_CHAN, N_STN, CAP), jnp.float32) ** shard_levels(splits[1], (2, N_STN, N_CHAN, N_STN, CAP), ((1, 32), (2, 8)), -0.2, 0.2), 0.0, 1.0),
        "query_dest": draw_query_dest(jax.random.fold_in(splits[8], 71), 0),
        "positions": jnp.clip(jax.random.uniform(splits[3], (3, STATIONS), jnp.float32, -50.0, 50.0) * shard_levels(splits[3], (3, STATIONS), ((1, 32),), -0.4, 0.0), -50.0, 50.0),
        "directions": jnp.clip(jax.random.uniform(splits[4], (3, SRC), jnp.float32, -0.7, 0.7), -0.7, 0.7),
        "freq_ratio": jnp.clip(jnp.exp(math.log(1.4) - 0.6931472 * jax.random.uniform(splits[5], (CHANNELS,), jnp.float32) ** shard_levels(splits[5], (CHANNELS,), ((0, 8),), -0.2, 0.2)), 0.7, 1.4),
        "source_flux": jnp.clip(jnp.exp(jax.random.uniform(splits[6], (SRC,), jnp.float32, math.log(0.2), math.log(5.0))), 0.2, 5.0),
        "spectral_index": jnp.clip(jax.random.uniform(splits[7], (SRC,), jnp.float32, -1.5, 0.5), -1.5, 0.5),
    }


TWO_PI = 2.0 * math.pi

def interpolate(values, coords, strip_rows, tile_cols, offsets):
    row_pos = coords[0] * (strip_rows - 1)
    col_pos = coords[1] * (tile_cols - 1)
    row_low = jnp.clip(jnp.floor(row_pos), 0.0, strip_rows - 2.0)
    col_low = jnp.clip(jnp.floor(col_pos), 0.0, tile_cols - 2.0)
    frac_y = row_pos - row_low
    frac_x = col_pos - col_low
    corner = offsets + row_low.astype(jnp.int32) * tile_cols + col_low.astype(jnp.int32)
    lower_pair = (1.0 - frac_x) * values[corner] + frac_x * values[corner + 1]
    upper_pair = (1.0 - frac_x) * values[corner + tile_cols] + frac_x * values[corner + tile_cols + 1]
    return (1.0 - frac_y) * lower_pair + frac_y * upper_pair

def make_phasors(station_rows, iono_rows, directions, freq_ratio):
    delays = station_rows[:, 0:1] * directions[0][None, :] + station_rows[:, 1:2] * directions[1][None, :]
    delays = delays + station_rows[:, 2:3] * directions[2][None, :]
    angles = (TWO_PI * freq_ratio)[None, :, None] * delays[:, None, :] + iono_rows[:, None, :] / freq_ratio[None, :, None]
    return jnp.concatenate([jnp.cos(angles), jnp.sin(angles)], axis=-1).astype(jnp.bfloat16)

def spectrum(source_flux, spectral_index, freq_ratio, count):
    return source_flux[None, :] * jnp.exp(spectral_index[None, :] * jnp.log(freq_ratio)[:, None]) / math.sqrt(count)

def weight_rows(phasors, intensity):
    sources = intensity.shape[1]
    real_part = (phasors[:, :, :sources].astype(jnp.float32) * intensity[None]).astype(jnp.bfloat16)
    imag_part = (phasors[:, :, sources:].astype(jnp.float32) * intensity[None]).astype(jnp.bfloat16)
    upper_rows = jnp.concatenate([real_part, imag_part], axis=-1)
    lower_rows = jnp.concatenate([imag_part, -real_part], axis=-1)
    return jnp.concatenate([upper_rows, lower_rows], axis=0)

def reference(screen, pierce_coords, query_dest, positions, directions, freq_ratio, source_flux, spectral_index):
    strip_rows = TILES_DEV * TILE
    values = screen.reshape(-1)
    owners = jnp.arange(N_STN, dtype=jnp.int32)[None, None, :, None] * (strip_rows * TILE)
    sampled = interpolate(values, pierce_coords, strip_rows, TILE, owners)
    blocks = N_STN * N_CHAN
    block_ids = jnp.broadcast_to(jnp.arange(blocks, dtype=jnp.int32).reshape(N_STN, N_CHAN, 1, 1), query_dest.shape)
    buffer = jnp.zeros((blocks, QUERIES + 1), jnp.float32).at[block_ids, query_dest].set(sampled.astype(jnp.float32))
    iono_phase = buffer[:, :QUERIES].reshape(N_STN, N_CHAN, STN_DEV, SRCC).transpose(0, 2, 1, 3).reshape(STATIONS, SRC)
    phasors = make_phasors(positions.T, iono_phase, directions, freq_ratio)
    intensity = spectrum(source_flux, spectral_index, freq_ratio, SRC)
    weighted = weight_rows(phasors, intensity)

    def per_channel(operands):
        return jnp.dot(operands[0], operands[1].T, preferred_element_type=jnp.float32)
    result = lax.map(per_channel, (weighted.transpose(1, 0, 2), phasors.transpose(1, 0, 2)))
    visible = result.reshape(CHANNELS, 2, STATIONS, STATIONS)
    cross_only = jnp.arange(STATIONS)[:, None] != jnp.arange(STATIONS)[None, :]
    return jnp.where(cross_only[None, None], visible, jnp.zeros_like(visible))
```

```python
import functools
import math

import jax
import jax.numpy as jnp
from jax import lax
from jax.experimental import pallas as pl
from jax.experimental.pallas import tpu as pltpu
from jax.sharding import PartitionSpec as P

MESH = pl.DeviceIdType.MESH
TWO_PI = 2.0 * math.pi
VMEM = pltpu.VMEM
NT = (((1,), (1,)), ((), ()))

SIN_COEFS = (4.4428679, -7.30744342, 3.59478808, -0.78437402)
COS_COEFS = (1.41420408, -6.97764206, 5.71523838, -1.72834863)


def half_turn_phasor(turns):
    r = turns - jnp.round(turns)
    u = r * r
    s = r * (SIN_COEFS[0] + u * (SIN_COEFS[1] + u * (SIN_COEFS[2] + u * SIN_COEFS[3])))
    c = COS_COEFS[0] + u * (COS_COEFS[1] + u * (COS_COEFS[2] + u * COS_COEFS[3]))
    return 1.0 - s * s, s * c


def exchange_kernel(n, msg_ref, out_ref, local_sem, send_sem, recv_sem):
    g = lax.axis_index("stn")
    c = lax.axis_index("chan")
    barrier = pltpu.get_barrier_semaphore()
    for k in range(1, n):
        pl.semaphore_signal(barrier, inc=1, device_id=(lax.rem(g + k, n), c), device_id_type=MESH)
    own = pltpu.make_async_copy(msg_ref.at[:, pl.ds(g, 1)], out_ref.at[:, pl.ds(g, 1)], local_sem)
    own.start()
    pl.semaphore_wait(barrier, n - 1)
    copies = []
    for k in range(1, n):
        to = lax.rem(g + k, n)
        copy = pltpu.make_async_remote_copy(
            src_ref=msg_ref.at[:, pl.ds(to, 1)],
            dst_ref=out_ref.at[:, pl.ds(g, 1)],
            send_sem=send_sem.at[k],
            recv_sem=recv_sem.at[k],
            device_id=(to, c),
            device_id_type=MESH,
        )
        copy.start()
        copies.append(copy)
    own.wait()
    for copy in copies:
        copy.wait()


def exchange(msg, n):
    return pl.pallas_call(
        functools.partial(exchange_kernel, n),
        out_shape=jax.ShapeDtypeStruct(msg.shape, msg.dtype),
        in_specs=[pl.BlockSpec(memory_space=VMEM)],
        out_specs=pl.BlockSpec(memory_space=VMEM),
        scratch_shapes=[
            pltpu.SemaphoreType.DMA,
            pltpu.SemaphoreType.DMA((n,)),
            pltpu.SemaphoreType.DMA((n,)),
        ],
        compiler_params=pltpu.CompilerParams(collective_id=0, has_side_effects=True),
        name="exchange",
    )(msg)


def lookup_kernel(addr_ref, frac_ref, screen_ref, out_ref, wide, stage):
    rows = screen_ref.shape[0]
    step = 64

    def widen(i, carry):
        here = pl.ds(pl.multiple_of(i * step, step), step)
        lane = lax.broadcasted_iota(jnp.int32, (step, 128), 1)
        tiles = [screen_ref[here, m * 128 : (m + 1) * 128] for m in range(4)]
        wide[here, :] = tiles[0]
        for b in range(1, 5):
            mixed = tiles[3] if b == 4 else jnp.where(lane >= 128 - b, tiles[b - 1], tiles[b])
            wide[pl.ds(pl.multiple_of(b * rows + i * step, step), step), :] = pltpu.roll(mixed, b, 1)
        return carry

    lax.fori_loop(0, rows // step, widen, 0)
    sub = lax.broadcasted_iota(jnp.int32, (128, 128), 0).astype(jnp.float32)

    def group(g, carry):
        for j in range(128):
            a = addr_ref[g, j]
            stage[2 * j : 2 * j + 2, :] = wide[pl.ds(a, 2), :]
        low = stage[pl.ds(0, 128, stride=2), :].T
        high = stage[pl.ds(1, 128, stride=2), :].T
        fy = frac_ref[0, pl.ds(g, 1), :]
        x = frac_ref[1, pl.ds(g, 1), :]
        mixed = (1.0 - fy) * low + fy * high
        tent = jnp.maximum(1.0 - jnp.abs(sub - x), 0.0)
        out_ref[pl.ds(g, 1), :] = jnp.sum(mixed * tent, axis=0, keepdims=True)
        return carry

    lax.fori_loop(0, addr_ref.shape[0], group, 0)


def lookup(addr, frac, screen):
    rows = screen.shape[0]
    return pl.pallas_call(
        lookup_kernel,
        out_shape=jax.ShapeDtypeStruct(addr.shape, jnp.float32),
        in_specs=[
            pl.BlockSpec(memory_space=pltpu.SMEM),
            pl.BlockSpec(memory_space=VMEM),
            pl.BlockSpec(memory_space=VMEM),
        ],
        out_specs=pl.BlockSpec(memory_space=VMEM),
        scratch_shapes=[VMEM((5 * rows, 128), jnp.float32), VMEM((256, 128), jnp.float32)],
        compiler_params=pltpu.CompilerParams(vmem_limit_bytes=32 << 20),
        name="lookup",
    )(addr, frac, screen)


def phases_kernel(
    sampled_ref, dest_ref, out_ref, back, blocks, local_sem, back_send, back_recv, z_send, z_recv,
    xy_send, xy_recv, core_send, core_recv,
):
    g = lax.axis_index("stn")
    c = lax.axis_index("chan")
    n = 32
    z = g // 4
    xh = (g // 2) % 2
    core = g % 2
    sibling = g + 1 - 2 * core
    barrier = pltpu.get_barrier_semaphore()
    xy = [(h, m) for h in range(2) for m in range(8) if (h, m) != (0, 0)]

    def xy_peer(h, m):
        return (z * 4 + ((xh + h) % 2) * 2 + core, (c + m) % 8)

    for k in range(1, n):
        pl.semaphore_signal(barrier, inc=1, device_id=((g + k) % n, c), device_id_type=MESH)
    for h, m in xy:
        if m:
            pl.semaphore_signal(barrier, inc=1, device_id=xy_peer(h, m), device_id_type=MESH)
    own = pltpu.make_async_copy(sampled_ref.at[pl.ds(g, 1)], back.at[pl.ds(g, 1)], local_sem)
    own.start()
    pl.semaphore_wait(barrier, n - 1 + 14)
    returns = []
    for k in range(1, n):
        to = (g + k) % n
        copy = pltpu.make_async_remote_copy(
            src_ref=sampled_ref.at[pl.ds(to, 1)],
            dst_ref=back.at[pl.ds(g, 1)],
            send_sem=back_send.at[k],
            recv_sem=back_recv.at[k],
            device_id=(to, c),
            device_id_type=MESH,
        )
        copy.start()
        returns.append(copy)
    own.wait()
    for copy in returns:
        copy.wait_recv()

    total = jnp.zeros((24, 128), jnp.float32)
    row_id = lax.broadcasted_iota(jnp.int32, (8, 128), 0)
    lane_id = lax.broadcasted_iota(jnp.int32, (128, 128), 0)
    for j in range(0, n, 2):
        left, right = [], []
        for o in (j, j + 1):
            v = back[o : o + 1, :]
            dest = dest_ref[o : o + 1, :]
            a = (dest // 64) % 8
            b = (dest // 512) * 64 + dest % 64
            hi = v.astype(jnp.bfloat16).astype(jnp.float32)
            mid = (v - hi).astype(jnp.bfloat16).astype(jnp.float32)
            lo = v - hi - mid
            hit = row_id == a
            left.append(
                jnp.concatenate([jnp.where(hit, part, 0.0) for part in (hi, mid, lo)], axis=0)
            )
            right.append(jnp.where(lane_id == b, 1.0, 0.0))
        total = total + lax.dot_general(
            jnp.concatenate(left, axis=1).astype(jnp.bfloat16),
            jnp.concatenate(right, axis=1).astype(jnp.bfloat16),
            NT,
            preferred_element_type=jnp.float32,
        )
    mine = (total[0:8] + total[8:16] + total[16:24]) * (1.0 / TWO_PI)
    blocks[core, xh, c, z] = mine

    z_copies = []
    for k in range(1, 8):
        copy = pltpu.make_async_remote_copy(
            src_ref=blocks.at[core, xh, c, z],
            dst_ref=blocks.at[core, xh, c, z],
            send_sem=z_send.at[k],
            recv_sem=z_recv.at[k],
            device_id=(((z + k) % 8) * 4 + xh * 2 + core, c),
            device_id_type=MESH,
        )
        copy.start()
        z_copies.append(copy)
    for copy in z_copies:
        copy.wait_recv()

    xy_copies = {}
    for h, m in xy:
        copy = pltpu.make_async_remote_copy(
            src_ref=blocks.at[core, xh, c],
            dst_ref=blocks.at[core, xh, c],
            send_sem=xy_send.at[h * 8 + m],
            recv_sem=xy_recv.at[h * 8 + m],
            device_id=xy_peer(h, m),
            device_id_type=MESH,
        )
        copy.start()
        xy_copies[h, m] = copy

    core_copies = []
    for h, m in [(0, 0)] + xy:
        if (h, m) != (0, 0):
            xy_copies[h, m].wait_recv()
        block = blocks.at[core, (xh + 2 - h) % 2, (c + 8 - m) % 8]
        copy = pltpu.make_async_remote_copy(
            src_ref=block,
            dst_ref=block,
            send_sem=core_send.at[h * 8 + m],
            recv_sem=core_recv.at[h * 8 + m],
            device_id=(sibling, c),
            device_id_type=MESH,
        )
        copy.start()
        core_copies.append(copy)
    for copy in core_copies:
        copy.wait()
    for copy in returns + z_copies + list(xy_copies.values()):
        copy.wait_send()

    lane = lax.broadcasted_iota(jnp.int32, (8, 128), 1)

    def spread(zz, carry):
        for group in range(4):
            kk, hh = group % 2, group // 2
            for m in range(4):
                even = blocks[kk, hh, 2 * m, zz]
                odd = blocks[kk, hh, 2 * m + 1, zz]
                first = pl.multiple_of((zz * 4 + group) * 16, 16)
                cols = slice(m * 128, (m + 1) * 128)
                out_ref[pl.ds(first, 8), cols] = jnp.where(lane < 64, even, pltpu.roll(odd, 64, 1))
                out_ref[pl.ds(first + 8, 8), cols] = jnp.where(
                    lane < 64, pltpu.roll(even, 64, 1), odd
                )
        return carry

    lax.fori_loop(0, 8, spread, 0)


def gather_phases(sampled, dest, stations, sources):
    dma = pltpu.SemaphoreType.DMA
    return pl.pallas_call(
        phases_kernel,
        out_shape=jax.ShapeDtypeStruct((stations, sources), jnp.float32),
        in_specs=[pl.BlockSpec(memory_space=VMEM)] * 2,
        out_specs=pl.BlockSpec(memory_space=VMEM),
        scratch_shapes=[
            VMEM((32, 128), jnp.float32),
            VMEM((2, 2, 8, 8, 8, 128), jnp.float32),
            dma,
            dma((32,)), dma((32,)),
            dma((8,)), dma((8,)),
            dma((16,)), dma((16,)),
            dma((16,)), dma((16,)),
        ],
        compiler_params=pltpu.CompilerParams(
            collective_id=1, has_side_effects=True, vmem_limit_bytes=32 << 20
        ),
        name="phases",
    )(sampled, dest)


def visibility_kernel(
    msg_ref, phase_ref, directions_ref, freq_ref, flux_ref, index_ref, out_ref, delay, phasor
):
    stations, sources = phase_ref.shape
    g = lax.axis_index("stn")
    f = pl.program_id(0)
    tile = 16

    @pl.when(f == 0)
    def _():
        turned = msg_ref[2].T
        for block in range(stations // tile):
            cols = [turned[j * 16 : (j + 1) * 16, block : block + 1] for j in range(3)]
            d = (cols[0] * directions_ref[0:1, :] + cols[1] * directions_ref[1:2, :]) + cols[
                2
            ] * directions_ref[2:3, :]
            delay[block * tile : (block + 1) * tile, :] = d

    freq = freq_ref[f]
    wide = jnp.full((1, sources), freq, jnp.float32)
    inverse = 1.0 / wide
    intensity = (
        flux_ref[...] * jnp.exp(index_ref[...] * jnp.log(wide)) * (1.0 / math.sqrt(sources))
    )

    def phasors(here):
        turns = freq * delay[here, :] + inverse * phase_ref[here, :]
        return half_turn_phasor(turns)

    re, im = phasors(pl.ds(pl.multiple_of(g * 16, 16), 16))
    re = (re * intensity).astype(jnp.bfloat16)
    im = (im * intensity).astype(jnp.bfloat16)
    left = jnp.concatenate(
        [jnp.concatenate([re, im], axis=1), jnp.concatenate([im, -re], axis=1)], axis=0
    )
    rows = lax.broadcasted_iota(jnp.int32, (16, 256), 0) + g * 16
    cols = lax.broadcasted_iota(jnp.int32, (16, 256), 1)
    for part in range(stations // 256):
        for t in range(256 // tile):
            first = part * 256 + t * tile
            re, im = phasors(slice(first, first + tile))
            phasor[first : first + tile, :sources] = re.astype(jnp.bfloat16)
            phasor[first : first + tile, sources:] = im.astype(jnp.bfloat16)
        here = slice(part * 256, (part + 1) * 256)
        result = lax.dot_general(left, phasor[here, :], NT, preferred_element_type=jnp.float32)
        cross = rows != cols + part * 256
        out_ref[0, 0, :, here] = jnp.where(cross, result[:16], 0.0)
        out_ref[0, 1, :, here] = jnp.where(cross, result[16:], 0.0)


def visibilities(msg, phases, directions, freq_ratio, flux, index):
    stations, sources = phases.shape
    channels = freq_ratio.shape[0]
    vmem = pl.BlockSpec(memory_space=VMEM)
    return pl.pallas_call(
        visibility_kernel,
        grid=(channels,),
        out_shape=jax.ShapeDtypeStruct((channels, 2, 16, stations), jnp.float32),
        in_specs=[vmem, vmem, vmem, pl.BlockSpec(memory_space=pltpu.SMEM), vmem, vmem],
        out_specs=pl.BlockSpec((1, 2, 16, stations), lambda f: (f, 0, 0, 0)),
        scratch_shapes=[
            VMEM((stations, sources), jnp.float32),
            VMEM((stations, 2 * sources), jnp.bfloat16),
        ],
        compiler_params=pltpu.CompilerParams(vmem_limit_bytes=32 << 20),
        name="visibilities",
    )(msg, phases, directions, freq_ratio, flux, index)


def body(
    screen, pierce_coords, query_dest, positions, directions, freq_ratio, source_flux, spectral_index
):
    groups = lax.axis_size("stn")
    tile_cols = screen.shape[2]
    strip = screen.reshape(-1, tile_cols)
    capacity = query_dest.shape[3]
    coords = pierce_coords.reshape(2, groups, capacity)
    station_row = jnp.pad(positions.reshape(1, 1, -1), ((0, 0), (0, 0), (0, capacity - positions.size)))
    msg = jnp.concatenate(
        [coords, jnp.broadcast_to(station_row, (1, groups, capacity))], axis=0
    )
    msg = exchange(msg, groups)

    row_pos = msg[0] * (strip.shape[0] - 1)
    col_pos = msg[1] * (tile_cols - 1)
    row_low = jnp.clip(jnp.floor(row_pos), 0.0, strip.shape[0] - 2.0)
    col_low = jnp.clip(jnp.floor(col_pos), 0.0, tile_cols - 2.0)
    column = col_low.astype(jnp.int32)
    part = column // 127
    addr = part * strip.shape[0] + row_low.astype(jnp.int32)
    frac = jnp.stack([row_pos - row_low, col_pos - (part * 127).astype(jnp.float32)])
    sampled = lookup(addr, frac, strip)

    stations = positions.shape[1] * groups
    phases = gather_phases(
        sampled, query_dest.reshape(groups, capacity), stations, source_flux.shape[0]
    )
    return visibilities(
        msg, phases, directions, freq_ratio, source_flux.reshape(1, -1), spectral_index.reshape(1, -1)
    )


def solution(mesh):
    in_specs = (
        P("stn", None, None),
        P(None, "stn", "chan", None, None),
        P("stn", "chan", None, None),
        P(None, "stn"),
        P(),
        P("chan"),
        P(),
        P(),
    )
    out_specs = P("chan", None, "stn", None)
    return jax.shard_map(body, mesh=mesh, in_specs=in_specs, out_specs=out_specs, check_vma=False)
```

```python
import functools
import math

import jax
import jax.numpy as jnp
from jax import lax
from jax.experimental import pallas as pl
from jax.experimental.pallas import tpu as pltpu
from jax.sharding import PartitionSpec as P

MESH = pl.DeviceIdType.MESH
TWO_PI = 2.0 * math.pi
VMEM = pltpu.VMEM
NT = (((1,), (1,)), ((), ()))

SIN_COEFS = (4.4428679, -7.30744342, 3.59478808, -0.78437402)
COS_COEFS = (1.41420408, -6.97764206, 5.71523838, -1.72834863)


def half_turn_phasor(turns):
    r = turns - jnp.round(turns)
    u = r * r
    s = r * (SIN_COEFS[0] + u * (SIN_COEFS[1] + u * (SIN_COEFS[2] + u * SIN_COEFS[3])))
    c = COS_COEFS[0] + u * (COS_COEFS[1] + u * (COS_COEFS[2] + u * COS_COEFS[3]))
    return 1.0 - s * s, s * c


def whole_kernel(
    coords_hbm, cells_hbm, positions_hbm, dest_hbm, directions_hbm, screen_hbm, freq_hbm, flux_hbm, index_hbm,
    out_ref,
    strip, coords_ref, msg, got, cells_ref, frac, addr_smem, wide, stage, sampled, back, blocks,
    positions_ref, dest_ref, directions_ref, freq_ref, flux_ref, index_ref,
    phase_ref, delay_ref, phasor, theirs,
    screen_sem, in_sem, local_sem, addr_sem, ask_send, ask_recv, back_send, back_recv,
    z_send, z_recv, xy_send, xy_recv, core_send, core_recv, vis_send, vis_recv,
):
    g = lax.axis_index("stn")
    c = lax.axis_index("chan")
    n = 32
    z = g // 4
    xh = (g // 2) % 2
    core = g % 2
    sibling = g + 1 - 2 * core
    rows = strip.shape[0]
    barrier = pltpu.get_barrier_semaphore()
    xy = [(h, m) for h in range(2) for m in range(8) if (h, m) != (0, 0)]

    def xy_peer(h, m):
        return (z * 4 + ((xh + h) % 2) * 2 + core, (c + m) % 8)

    def stn_peer(k):
        return ((g + k) % n, c)

    screen_copy = pltpu.make_async_copy(screen_hbm, strip, screen_sem)
    coords_copy = pltpu.make_async_copy(coords_hbm, coords_ref, in_sem.at[0])
    cells_copy = pltpu.make_async_copy(cells_hbm, msg.at[0], in_sem.at[7])
    positions_copy = pltpu.make_async_copy(positions_hbm, positions_ref, in_sem.at[1])
    later = [
        pltpu.make_async_copy(source, target, in_sem.at[2 + i])
        for i, (source, target) in enumerate(
            (
                (dest_hbm, dest_ref),
                (directions_hbm, directions_ref),
                (freq_hbm, freq_ref),
                (flux_hbm, flux_ref),
                (index_hbm, index_ref),
            )
        )
    ]
    for copy in [coords_copy, cells_copy, positions_copy, screen_copy] + later:
        copy.start()
    for k in range(1, n):
        pl.semaphore_signal(barrier, inc=1, device_id=stn_peer(k), device_id_type=MESH)
    for h, m in xy:
        if m:
            pl.semaphore_signal(barrier, inc=1, device_id=xy_peer(h, m), device_id_type=MESH)
    positions_copy.wait()
    station_row = jnp.concatenate(
        [positions_ref[j : j + 1, :] for j in range(3)] + [jnp.zeros((1, 80), jnp.float32)], axis=1
    )
    msg[3] = jnp.broadcast_to((station_row * 2.0**24).astype(jnp.int32), (n, 128))
    coords_copy.wait()
    cells_copy.wait()
    cell = msg[0]
    low_row = (cell % rows).astype(jnp.float32)
    low_col = (cell // rows * 127).astype(jnp.float32)
    msg[1] = ((coords_ref[0] * (rows - 1) - low_row) * 2.0**24).astype(jnp.int32)
    msg[2] = ((coords_ref[1] * (strip.shape[1] - 1) - low_col) * 2.0**23).astype(jnp.int32)
    own = pltpu.make_async_copy(msg.at[:, pl.ds(g, 1)], got.at[:, pl.ds(g, 1)], local_sem.at[0])
    own.start()
    pl.semaphore_wait(barrier, n - 1 + 14)

    def ask(k):
        return pltpu.make_async_remote_copy(
            src_ref=msg.at[:, pl.ds((g + k) % n, 1)],
            dst_ref=got.at[:, pl.ds(g, 1)],
            send_sem=ask_send.at[k],
            recv_sem=ask_recv.at[k],
            device_id=stn_peer(k),
            device_id_type=MESH,
        )

    for k in range(1, n):
        ask(k).start()

    screen_copy.wait()
    step = 64

    def widen(i, carry):
        here = pl.ds(pl.multiple_of(i * step, step), step)
        lane = lax.broadcasted_iota(jnp.int32, (step, 128), 1)
        tiles = [strip[here, m * 128 : (m + 1) * 128] for m in range(4)]
        wide[here, :] = tiles[0]
        for b in range(1, 5):
            mixed = tiles[3] if b == 4 else jnp.where(lane >= 128 - b, tiles[b - 1], tiles[b])
            wide[pl.ds(pl.multiple_of(b * rows + i * step, step), step), :] = pltpu.roll(mixed, b, 1)
        return carry

    lax.fori_loop(0, rows // step, widen, 0)

    for copy in later:
        copy.wait()
    own.wait()
    for k in range(1, n):
        ask(k).wait_recv()
    cells_ref[...] = jnp.clip(got[0], 0, 5 * rows - 2)
    to_smem = pltpu.make_async_copy(cells_ref, addr_smem, addr_sem)
    to_smem.start()
    frac[0] = got[1].astype(jnp.float32) * 2.0**-24
    frac[1] = got[2].astype(jnp.float32) * 2.0**-23
    to_smem.wait()

    sub = lax.broadcasted_iota(jnp.int32, (128, 128), 0).astype(jnp.float32)

    def answer(k):
        return pltpu.make_async_remote_copy(
            src_ref=sampled.at[pl.ds((g + k) % n, 1)],
            dst_ref=back.at[pl.ds(g, 1)],
            send_sem=back_send.at[k],
            recv_sem=back_recv.at[k],
            device_id=stn_peer(k),
            device_id_type=MESH,
        )

    def look_up(k, carry):
        to = (g + k) % n
        for j in range(128):
            stage[2 * j : 2 * j + 2, :] = wide[pl.ds(addr_smem[to, j], 2), :]
        low = stage[pl.ds(0, 128, stride=2), :].T
        high = stage[pl.ds(1, 128, stride=2), :].T
        fy = frac[0, pl.ds(to, 1), :]
        mixed = (1.0 - fy) * low + fy * high
        tent = jnp.maximum(1.0 - jnp.abs(sub - frac[1, pl.ds(to, 1), :]), 0.0)
        sampled[pl.ds(to, 1), :] = jnp.sum(mixed * tent, axis=0, keepdims=True)

        @pl.when(k < n)
        def _():
            answer(k).start()

        return carry

    lax.fori_loop(1, n + 1, look_up, 0)
    keep = pltpu.make_async_copy(sampled.at[pl.ds(g, 1)], back.at[pl.ds(g, 1)], local_sem.at[1])
    keep.start()
    keep.wait()
    for k in range(1, n):
        answer(k).wait_recv()

    total = jnp.zeros((24, 128), jnp.float32)
    row_id = lax.broadcasted_iota(jnp.int32, (8, 128), 0)
    lane_id = lax.broadcasted_iota(jnp.int32, (128, 128), 0)
    for j in range(0, n, 2):
        left, right = [], []
        for o in (j, j + 1):
            v = back[o : o + 1, :]
            dest = dest_ref[o : o + 1, :]
            a = (dest // 64) % 8
            b = (dest // 512) * 64 + dest % 64
            hi = v.astype(jnp.bfloat16).astype(jnp.float32)
            mid = (v - hi).astype(jnp.bfloat16).astype(jnp.float32)
            lo = v - hi - mid
            hit = row_id == a
            left.append(
                jnp.concatenate([jnp.where(hit, part, 0.0) for part in (hi, mid, lo)], axis=0)
            )
            right.append(jnp.where(lane_id == b, 1.0, 0.0))
        total = total + lax.dot_general(
            jnp.concatenate(left, axis=1).astype(jnp.bfloat16),
            jnp.concatenate(right, axis=1).astype(jnp.bfloat16),
            NT,
            preferred_element_type=jnp.float32,
        )
    mine = (total[0:8] + total[8:16] + total[16:24]) * (1.0 / TWO_PI)
    blocks[core, xh, c, z] = mine

    z_copies = []
    for k in range(1, 8):
        copy = pltpu.make_async_remote_copy(
            src_ref=blocks.at[core, xh, c, z],
            dst_ref=blocks.at[core, xh, c, z],
            send_sem=z_send.at[k],
            recv_sem=z_recv.at[k],
            device_id=(((z + k) % 8) * 4 + xh * 2 + core, c),
            device_id_type=MESH,
        )
        copy.start()
        z_copies.append(copy)

    turned = (got[3].astype(jnp.float32) * 2.0**-24).T
    for block in range(n):
        cols = [turned[j * 16 : (j + 1) * 16, block : block + 1] for j in range(3)]
        delay_ref[block * 16 : (block + 1) * 16, :] = (
            cols[0] * directions_ref[0:1, :] + cols[1] * directions_ref[1:2, :]
        ) + cols[2] * directions_ref[2:3, :]

    for copy in z_copies:
        copy.wait_recv()

    xy_copies = {}
    for h, m in xy:
        copy = pltpu.make_async_remote_copy(
            src_ref=blocks.at[core, xh, c],
            dst_ref=blocks.at[core, xh, c],
            send_sem=xy_send.at[h * 8 + m],
            recv_sem=xy_recv.at[h * 8 + m],
            device_id=xy_peer(h, m),
            device_id_type=MESH,
        )
        copy.start()
        xy_copies[h, m] = copy

    core_copies = []
    for h, m in [(0, 0)] + xy:
        if (h, m) != (0, 0):
            xy_copies[h, m].wait_recv()
        block = blocks.at[core, (xh + 2 - h) % 2, (c + 8 - m) % 8]
        copy = pltpu.make_async_remote_copy(
            src_ref=block,
            dst_ref=block,
            send_sem=core_send.at[h * 8 + m],
            recv_sem=core_recv.at[h * 8 + m],
            device_id=(sibling, c),
            device_id_type=MESH,
        )
        copy.start()
        core_copies.append(copy)
    for copy in core_copies:
        copy.wait()
    for k in range(1, n):
        ask(k).wait_send()
        answer(k).wait_send()
    for copy in z_copies + list(xy_copies.values()):
        copy.wait_send()

    lane = lax.broadcasted_iota(jnp.int32, (8, 128), 1)

    def spread(zz, carry):
        for group in range(4):
            kk, hh = group % 2, group // 2
            for m in range(4):
                even = blocks[kk, hh, 2 * m, zz]
                odd = blocks[kk, hh, 2 * m + 1, zz]
                first = pl.multiple_of((zz * 4 + group) * 16, 16)
                cols = slice(m * 128, (m + 1) * 128)
                phase_ref[pl.ds(first, 8), cols] = jnp.where(lane < 64, even, pltpu.roll(odd, 64, 1))
                phase_ref[pl.ds(first + 8, 8), cols] = jnp.where(
                    lane < 64, pltpu.roll(even, 64, 1), odd
                )
        return carry

    lax.fori_loop(0, 8, spread, 0)

    stations, sources = phase_ref.shape
    half = freq_ref.shape[0] // 2
    tile = 16
    def send(i):
        return pltpu.make_async_remote_copy(
            src_ref=theirs.at[pl.ds(2 * i, 2)],
            dst_ref=out_ref.at[pl.ds(core * half + 2 * i, 2)],
            send_sem=vis_send.at[i],
            recv_sem=vis_recv.at[i],
            device_id=(sibling, c),
            device_id_type=MESH,
        )

    def pair(i, carry):
        for which in range(2):
            f = core * half + 2 * i + which
            freq = freq_ref[f]
            wide = jnp.full((1, sources), freq, jnp.float32)
            inverse = 1.0 / wide
            intensity = (
                flux_ref[...] * jnp.exp(index_ref[...] * jnp.log(wide)) * (1.0 / math.sqrt(sources))
            )

            def phasors(here):
                return half_turn_phasor(freq * delay_ref[here, :] + inverse * phase_ref[here, :])

            upper, lower = [], []
            for group in (g, sibling):
                re, im = phasors(pl.ds(pl.multiple_of(group * 16, 16), 16))
                re = (re * intensity).astype(jnp.bfloat16)
                im = (im * intensity).astype(jnp.bfloat16)
                upper.append(jnp.concatenate([re, im], axis=1))
                lower.append(jnp.concatenate([im, -re], axis=1))
            left = jnp.concatenate(upper + lower, axis=0)
            for part in range(stations // 256):
                for t in range(256 // tile):
                    first = part * 256 + t * tile
                    re, im = phasors(slice(first, first + tile))
                    phasor[which, first : first + tile, :sources] = re.astype(jnp.bfloat16)
                    phasor[which, first : first + tile, sources:] = im.astype(jnp.bfloat16)
                here = slice(part * 256, (part + 1) * 256)
                result = lax.dot_general(
                    left, phasor[which, here, :], NT, preferred_element_type=jnp.float32
                ).astype(jnp.bfloat16)
                out_ref[f, 0, :, here] = result[0:16]
                theirs[2 * i + which, 0, :, here] = result[16:32]
                out_ref[f, 1, :, here] = result[32:48]
                theirs[2 * i + which, 1, :, here] = result[48:64]
        send(i).start()
        return carry

    lax.fori_loop(0, half // 2, pair, 0)
    for i in range(half // 2):
        send(i).wait()


def whole(coords, cells, positions, dest, directions, strip, freq, flux, index):
    dma = pltpu.SemaphoreType.DMA
    n = dest.shape[0]
    rows = strip.shape[0]
    channels = freq.shape[0]
    sources = flux.shape[1]
    stations = 16 * n
    bf16, f32 = jnp.bfloat16, jnp.float32
    return pl.pallas_call(
        whole_kernel,
        out_shape=jax.ShapeDtypeStruct((channels, 2, 16, stations), bf16),
        in_specs=[pl.BlockSpec(memory_space=pl.ANY)] * 9,
        out_specs=pl.BlockSpec(memory_space=VMEM),
        scratch_shapes=[
            VMEM(strip.shape, f32),
            VMEM((2, n, 128), f32),
            VMEM((4, n, 128), jnp.int32),
            VMEM((4, n, 128), jnp.int32),
            VMEM((n, 128), jnp.int32),
            VMEM((2, n, 128), f32),
            pltpu.SMEM((n, 128), jnp.int32),
            VMEM((5 * rows, 128), f32),
            VMEM((256, 128), f32),
            VMEM((n, 128), f32),
            VMEM((n, 128), f32),
            VMEM((2, 2, 8, 8, 8, 128), f32),
            VMEM(positions.shape, f32),
            VMEM(dest.shape, jnp.int32),
            VMEM(directions.shape, f32),
            pltpu.SMEM(freq.shape, f32),
            VMEM(flux.shape, f32),
            VMEM(index.shape, f32),
            VMEM((stations, sources), f32),
            VMEM((stations, sources), f32),
            VMEM((2, stations, 2 * sources), bf16),
            VMEM((channels // 2, 2, 16, stations), bf16),
            dma, dma((8,)), dma((2,)), dma,
            dma((32,)), dma((32,)),
            dma((33,)), dma((33,)),
            dma((8,)), dma((8,)),
            dma((16,)), dma((16,)),
            dma((16,)), dma((16,)),
            dma((channels // 4,)), dma((channels // 4,)),
        ],
        compiler_params=pltpu.CompilerParams(
            collective_id=1, has_side_effects=True, vmem_limit_bytes=60 << 20
        ),
        name="whole",
    )(coords, cells, positions, dest, directions, strip, freq, flux, index)


def body(
    screen, pierce_coords, query_dest, positions, directions, freq_ratio, source_flux, spectral_index
):
    groups = lax.axis_size("stn")
    capacity = query_dest.shape[3]
    stations = positions.shape[1] * groups
    rows = screen.shape[0] * screen.shape[1]
    cols = screen.shape[2]
    coords = pierce_coords.reshape(2, groups, capacity)
    row_low = jnp.clip(jnp.floor(coords[0] * (rows - 1)), 0.0, rows - 2.0).astype(jnp.int32)
    col_low = jnp.clip(jnp.floor(coords[1] * (cols - 1)), 0.0, cols - 2.0).astype(jnp.int32)
    visible = whole(
        coords,
        col_low // 127 * rows + row_low,
        positions,
        query_dest.reshape(groups, capacity),
        directions,
        screen.reshape(-1, screen.shape[2]),
        freq_ratio,
        source_flux.reshape(1, -1),
        spectral_index.reshape(1, -1),
    )
    own = lax.axis_index("stn") * positions.shape[1] + jnp.arange(positions.shape[1])
    cross_only = own[:, None] != jnp.arange(stations)[None, :]
    return jnp.where(cross_only[None, None], visible.astype(jnp.float32), 0.0)


def solution(mesh):
    in_specs = (
        P("stn", None, None),
        P(None, "stn", "chan", None, None),
        P("stn", "chan", None, None),
        P(None, "stn"),
        P(),
        P("chan"),
        P(),
        P(),
    )
    out_specs = P("chan", None, "stn", None)
    return jax.shard_map(body, mesh=mesh, in_specs=in_specs, out_specs=out_specs, check_vma=False)
```

```python
import functools
import math

import jax
import jax.numpy as jnp
from jax import lax
from jax.experimental import pallas as pl
from jax.experimental.pallas import tpu as pltpu
from jax.sharding import PartitionSpec as P

MESH = pl.DeviceIdType.MESH
TWO_PI = 2.0 * math.pi
VMEM = pltpu.VMEM
NT = (((1,), (1,)), ((), ()))

SIN_COEFS = (4.442852586664358, -7.306899436200296, 3.59017447630795, -0.7735545907233887)
PHASE_STEPS = 34000.0


def half_turn_phasor(turns):
    r = turns - jnp.round(turns)
    u = r * r
    s = r * (SIN_COEFS[0] + u * (SIN_COEFS[1] + u * (SIN_COEFS[2] + u * SIN_COEFS[3])))
    q = s * s
    w = jnp.maximum(2.0 - q, 1e-12)
    return 1.0 - q, s * (w * lax.rsqrt(w))


def whole_kernel(
    coords_hbm, cells_hbm, positions_hbm, dest_hbm, directions_hbm, screen_hbm, freq_hbm, flux_hbm, index_hbm,
    out_hbm,
    strip, coords_ref, msg, got, cells_ref, frac, addr_smem, wide, stage, sampled, back, blocks,
    positions_ref, dest_ref, directions_ref, freq_ref, flux_ref, index_ref,
    delays, delay, phase, phasor, intensity, inverse, total_ref,
    screen_sem, in_sem, local_sem, addr_sem, ask_send, ask_recv, back_send, back_recv,
    z_send, z_recv, xy_send, xy_recv, core_send, core_recv, vis_send, vis_recv, own_sem,
):
    g = lax.axis_index("stn")
    c = lax.axis_index("chan")
    n = 32
    z = g // 4
    xh = (g // 2) % 2
    core = g % 2
    sibling = g + 1 - 2 * core
    rows = strip.shape[0]
    barrier = pltpu.get_barrier_semaphore()
    y = c // 2
    xl = c % 2
    chip = [(0, 1), (1, 0), (1, 1)]
    xy = [(0, h, l) for h, l in chip]
    xy += [(dy, h, l) for dy in range(1, 4) for h, l in [(0, 0)] + chip]

    def xy_peer(dy, h, l):
        return (z * 4 + ((xh + h) % 2) * 2 + core, ((y + dy) % 4) * 2 + (xl + l) % 2)

    def stn_peer(k):
        return ((g + k) % n, c)

    screen_copy = pltpu.make_async_copy(screen_hbm, strip, screen_sem)
    coords_copy = pltpu.make_async_copy(coords_hbm, coords_ref, in_sem.at[0])
    cells_copy = pltpu.make_async_copy(cells_hbm, msg.at[0], in_sem.at[7])
    positions_copy = pltpu.make_async_copy(positions_hbm, positions_ref, in_sem.at[1])
    later = [
        pltpu.make_async_copy(source, target, in_sem.at[2 + i])
        for i, (source, target) in enumerate(
            (
                (dest_hbm, dest_ref),
                (directions_hbm, directions_ref),
                (freq_hbm, freq_ref),
                (flux_hbm, flux_ref),
                (index_hbm, index_ref),
            )
        )
    ]
    for copy in [coords_copy, cells_copy, positions_copy, screen_copy] + later:
        copy.start()
    for k in range(1, n):
        pl.semaphore_signal(barrier, inc=1, device_id=stn_peer(k), device_id_type=MESH)
    for dy, h, l in xy:
        if dy or l:
            pl.semaphore_signal(barrier, inc=1, device_id=xy_peer(dy, h, l), device_id_type=MESH)
    positions_copy.wait()
    station_row = jnp.concatenate(
        [positions_ref[j : j + 1, :] for j in range(3)] + [jnp.zeros((1, 80), jnp.float32)], axis=1
    )
    msg[3] = jnp.broadcast_to((station_row * 2.0**24).astype(jnp.int32), (n, 128))
    coords_copy.wait()
    cells_copy.wait()
    cell = msg[0]
    low_row = (cell % rows).astype(jnp.float32)
    low_col = (cell // rows * 127).astype(jnp.float32)
    msg[1] = ((coords_ref[0] * (rows - 1) - low_row) * 2.0**24).astype(jnp.int32)
    msg[2] = ((coords_ref[1] * (strip.shape[1] - 1) - low_col) * 2.0**23).astype(jnp.int32)
    own = pltpu.make_async_copy(msg.at[:, pl.ds(g, 1)], got.at[:, pl.ds(g, 1)], local_sem.at[0])
    own.start()
    pl.semaphore_wait(barrier, n - 1 + 14)

    def ask(k):
        return pltpu.make_async_remote_copy(
            src_ref=msg.at[:, pl.ds((g + k) % n, 1)],
            dst_ref=got.at[:, pl.ds(g, 1)],
            send_sem=ask_send.at[k],
            recv_sem=ask_recv.at[k],
            device_id=stn_peer(k),
            device_id_type=MESH,
        )

    for k in range(1, n):
        ask(k).start()

    screen_copy.wait()
    step = 64

    def widen(i, carry):
        here = pl.ds(pl.multiple_of(i * step, step), step)
        lane = lax.broadcasted_iota(jnp.int32, (step, 128), 1)
        tiles = [strip[here, m * 128 : (m + 1) * 128] for m in range(4)]
        wide[here, :] = tiles[0]
        for b in range(1, 5):
            mixed = tiles[3] if b == 4 else jnp.where(lane >= 128 - b, tiles[b - 1], tiles[b])
            wide[pl.ds(pl.multiple_of(b * rows + i * step, step), step), :] = pltpu.roll(mixed, b, 1)
        return carry

    lax.fori_loop(0, rows // step, widen, 0)

    for copy in later:
        copy.wait()
    own.wait()
    for k in range(1, n):
        ask(k).wait_recv()
    cells_ref[...] = jnp.clip(got[0], 0, 5 * rows - 2)
    to_smem = pltpu.make_async_copy(cells_ref, addr_smem, addr_sem)
    to_smem.start()
    frac[0] = got[1].astype(jnp.float32) * 2.0**-24
    frac[1] = got[2].astype(jnp.float32) * 2.0**-23
    to_smem.wait()

    sub = lax.broadcasted_iota(jnp.int32, (128, 128), 0).astype(jnp.float32)

    def answer(k):
        return pltpu.make_async_remote_copy(
            src_ref=sampled.at[pl.ds((g + k) % n, 1)],
            dst_ref=back.at[pl.ds(g, 1)],
            send_sem=back_send.at[k],
            recv_sem=back_recv.at[k],
            device_id=stn_peer(k),
            device_id_type=MESH,
        )

    batch = stage.shape[0]

    def look_up(i, carry):
        for member in range(batch):
            k = 1 + i * batch + member
            to = (g + k) % n
            for j in range(128):
                stage[member, 2 * j : 2 * j + 2, :] = wide[pl.ds(addr_smem[to, j], 2), :]
            low = stage[member, pl.ds(0, 128, stride=2), :].T
            high = stage[member, pl.ds(1, 128, stride=2), :].T
            fy = frac[0, pl.ds(to, 1), :]
            mixed = (1.0 - fy) * low + fy * high
            tent = jnp.maximum(1.0 - jnp.abs(sub - frac[1, pl.ds(to, 1), :]), 0.0)
            sampled[pl.ds(to, 1), :] = jnp.sum(mixed * tent, axis=0, keepdims=True)

        for member in range(batch):
            k = 1 + i * batch + member

            @pl.when(k < n)
            def _(k=k):
                answer(k).start()

        return carry

    lax.fori_loop(0, n // batch, look_up, 0)
    keep = pltpu.make_async_copy(sampled.at[pl.ds(g, 1)], back.at[pl.ds(g, 1)], local_sem.at[1])
    keep.start()
    keep.wait()
    for k in range(1, n):
        answer(k).wait_recv()

    total = jnp.zeros((24, 128), jnp.float32)
    row_id = lax.broadcasted_iota(jnp.int32, (8, 128), 0)
    lane_id = lax.broadcasted_iota(jnp.int32, (128, 128), 0)
    for j in range(0, n, 2):
        left, right = [], []
        for o in (j, j + 1):
            v = back[o : o + 1, :]
            dest = dest_ref[o : o + 1, :]
            a = (dest // 64) % 8
            b = (dest // 512) * 64 + dest % 64
            hi = v.astype(jnp.bfloat16).astype(jnp.float32)
            mid = (v - hi).astype(jnp.bfloat16).astype(jnp.float32)
            lo = v - hi - mid
            hit = row_id == a
            left.append(
                jnp.concatenate([jnp.where(hit, part, 0.0) for part in (hi, mid, lo)], axis=0)
            )
            right.append(jnp.where(lane_id == b, 1.0, 0.0))
        total = total + lax.dot_general(
            jnp.concatenate(left, axis=1).astype(jnp.bfloat16),
            jnp.concatenate(right, axis=1).astype(jnp.bfloat16),
            NT,
            preferred_element_type=jnp.float32,
        )
    mine = jnp.round((total[0:8] + total[8:16] + total[16:24]) * (PHASE_STEPS / TWO_PI))
    mine = mine.astype(jnp.int32)
    own_rows = pl.ds(4 * z, 4)
    blocks[y, core, xh, xl, own_rows] = (mine[0:4] << 16) | (mine[4:8] & 0xFFFF)

    z_copies = []
    for k in range(1, 8):
        copy = pltpu.make_async_remote_copy(
            src_ref=blocks.at[y, core, xh, xl, own_rows],
            dst_ref=blocks.at[y, core, xh, xl, own_rows],
            send_sem=z_send.at[k],
            recv_sem=z_recv.at[k],
            device_id=(((z + k) % 8) * 4 + xh * 2 + core, c),
            device_id_type=MESH,
        )
        copy.start()
        z_copies.append(copy)

    turned = (got[3].astype(jnp.float32) * 2.0**-24).T
    for block in range(n):
        cols = [turned[j * 16 : (j + 1) * 16, block : block + 1] for j in range(3)]
        for m in range(4):
            lanes = slice(m * 128, (m + 1) * 128)
            delays[m, block * 16 : (block + 1) * 16, :] = (
                cols[0] * directions_ref[0:1, lanes] + cols[1] * directions_ref[1:2, lanes]
            ) + cols[2] * directions_ref[2:3, lanes]
    half = freq_ref.shape[0] // 2
    sources = flux_ref.shape[0] * 128

    def prepare(i, carry):
        freq = jnp.full((8, 128), freq_ref[core * half + i], jnp.float32)
        inverse[i] = (1.0 / PHASE_STEPS) / freq
        intensity[i] = (
            flux_ref[...]
            * jnp.exp(index_ref[...] * jnp.log(freq[0:4]))
            * (1.0 / math.sqrt(sources))
        )
        total_ref[i] = jnp.zeros(total_ref.shape[1:], jnp.float32)
        return carry

    lax.fori_loop(0, half, prepare, 0)

    for copy in z_copies:
        copy.wait_recv()

    xy_copies = {}
    for dy, h, l in xy:
        copy = pltpu.make_async_remote_copy(
            src_ref=blocks.at[y, core, xh, xl],
            dst_ref=blocks.at[y, core, xh, xl],
            send_sem=xy_send.at[dy * 4 + h * 2 + l],
            recv_sem=xy_recv.at[dy * 4 + h * 2 + l],
            device_id=xy_peer(dy, h, l),
            device_id_type=MESH,
        )
        copy.start()
        xy_copies[dy, h, l] = copy

    def to_sibling(k):
        block = blocks.at[(y + 4 - k) % 4, core]
        return pltpu.make_async_remote_copy(
            src_ref=block,
            dst_ref=block,
            send_sem=core_send.at[k],
            recv_sem=core_recv.at[k],
            device_id=(sibling, c),
            device_id_type=MESH,
        )

    for h, l in chip:
        xy_copies[0, h, l].wait_recv()
    to_sibling(0).start()

    lane = lax.broadcasted_iota(jnp.int32, (8, 128), 1)
    sublane = lax.broadcasted_iota(jnp.int32, (8, 128), 0)

    def spread(k):
        to_sibling(k).wait_recv()
        m = (y + 4 - k) % 4
        delay[...] = delays[m]
        for pair in range(4):
            here = slice(pair * 8, (pair + 1) * 8)
            for group in range(4):
                kk, hh = group % 2, group // 2
                high, low = [], []
                for words in (blocks[m, kk, hh, 0, here], blocks[m, kk, hh, 1, here]):
                    high.append((words >> 16).astype(jnp.float32))
                    low.append(((words << 16) >> 16).astype(jnp.float32))
                for which in range(2):
                    even, odd = [
                        jnp.where(sublane < 4, hi, pltpu.roll(lo, 4, 0))
                        if which == 0
                        else jnp.where(sublane < 4, pltpu.roll(hi, 4, 0), lo)
                        for hi, lo in zip(high, low)
                    ]
                    first = ((2 * pair + which) * 4 + group) * 16
                    phase[first : first + 8] = jnp.where(lane < 64, even, pltpu.roll(odd, 64, 1))
                    phase[first + 8 : first + 16] = jnp.where(
                        lane < 64, pltpu.roll(even, 64, 1), odd
                    )

    stations = phase.shape[0]
    tile = 16
    chip_rows = pl.ds(pl.multiple_of((g // 2) * 32, 32), 32)

    def add_channels(k, first, count):
        m = (y + 4 - k) % 4
        for j in range(count):
            f = first + j
            freq = freq_ref[core * half + f]
            inv = inverse[f, 0:1]

            def phasors(here):
                re, im = half_turn_phasor(freq * delay[here, :] + inv * phase[here, :])
                return re.astype(jnp.bfloat16), im.astype(jnp.bfloat16)

            re, im = phasors(chip_rows)
            weight = intensity[f, pl.ds(m, 1)]
            re = (re.astype(jnp.float32) * weight).astype(jnp.bfloat16)
            im = (im.astype(jnp.float32) * weight).astype(jnp.bfloat16)
            left = jnp.concatenate(
                [jnp.concatenate([re, im], axis=1), jnp.concatenate([im, -re], axis=1)], axis=0
            )
            for t in range(stations // tile):
                here = slice(t * tile, (t + 1) * tile)
                re, im = phasors(here)
                phasor[j, here, :128] = re
                phasor[j, here, 128:] = im
            result = lax.dot_general(left, phasor[j], NT, preferred_element_type=jnp.float32)
            total_ref[f] = total_ref[f] + result.reshape(total_ref.shape[1:])

    def send(i, count):
        here = pl.ds(i * count, count)
        there = pl.ds(core * half + i * count, count)
        return (
            pltpu.make_async_copy(total_ref.at[here, :, core], out_hbm.at[there], own_sem.at[i]),
            pltpu.make_async_remote_copy(
                src_ref=total_ref.at[here, :, 1 - core],
                dst_ref=out_hbm.at[there],
                send_sem=vis_send.at[i],
                recv_sem=vis_recv.at[i],
                device_id=(sibling, c),
                device_id_type=MESH,
            ),
        )

    def finish(i, count):
        lanes = pl.ds(pl.multiple_of((g // 8) * 128, 128), 128)
        row = lax.broadcasted_iota(jnp.int32, (2, 16, 128), 0) * 16
        row = row + lax.broadcasted_iota(jnp.int32, (2, 16, 128), 1) + ((g // 2) % 4) * 32
        cross = lax.broadcasted_iota(jnp.int32, (2, 16, 128), 2) != row
        for j in range(count):
            for part in range(2):
                block = total_ref[i * count + j, part, :, :, lanes]
                total_ref[i * count + j, part, :, :, lanes] = jnp.where(cross, block, 0.0)
        for copy in send(i, count):
            copy.start()

    batch = half // 2
    quarter = half // 4

    def chunk(i, carry):
        k = i // 2

        @pl.when(i % 2 == 0)
        def _():
            spread(k)

        add_channels(k, (i % 2) * batch, batch)

        @pl.when(i == 0)
        def _():
            for dy in range(1, 4):
                for h, l in [(0, 0)] + chip:
                    xy_copies[dy, h, l].wait_recv()
                to_sibling(dy).start()

        return carry

    lax.fori_loop(0, 7, chunk, 0)
    for i in range(2):
        finish(i, quarter)

    def last(i, carry):
        add_channels(3, i * quarter, quarter)
        finish(i, quarter)
        return carry

    lax.fori_loop(2, 4, last, 0)
    for k in range(1, n):
        ask(k).wait_send()
        answer(k).wait_send()
    for copy in z_copies + list(xy_copies.values()):
        copy.wait_send()
    for k in range(4):
        to_sibling(k).wait_send()
        for copy in send(k, quarter):
            copy.wait()


def whole(coords, cells, positions, dest, directions, strip, freq, flux, index):
    dma = pltpu.SemaphoreType.DMA
    n = dest.shape[0]
    rows = strip.shape[0]
    channels = freq.shape[0]
    half = channels // 2
    stations = 16 * n
    bf16, f32 = jnp.bfloat16, jnp.float32
    return pl.pallas_call(
        whole_kernel,
        out_shape=jax.ShapeDtypeStruct((channels, 2, 16, stations), f32),
        in_specs=[pl.BlockSpec(memory_space=pl.ANY)] * 9,
        out_specs=pl.BlockSpec(memory_space=pl.ANY),
        scratch_shapes=[
            VMEM(strip.shape, f32),
            VMEM((2, n, 128), f32),
            VMEM((4, n, 128), jnp.int32),
            VMEM((4, n, 128), jnp.int32),
            VMEM((n, 128), jnp.int32),
            VMEM((2, n, 128), f32),
            pltpu.SMEM((n, 128), jnp.int32),
            VMEM((5 * rows, 128), f32),
            VMEM((4, 256, 128), f32),
            VMEM((n, 128), f32),
            VMEM((n, 128), f32),
            VMEM((4, 2, 2, 2, 32, 128), jnp.int32),
            VMEM(positions.shape, f32),
            VMEM(dest.shape, jnp.int32),
            VMEM(directions.shape, f32),
            pltpu.SMEM(freq.shape, f32),
            VMEM(flux.shape, f32),
            VMEM(index.shape, f32),
            VMEM((4, stations, 128), f32),
            VMEM((stations, 128), f32),
            VMEM((stations, 128), f32),
            VMEM((half // 2, stations, 256), bf16),
            VMEM((half, 4, 128), f32),
            VMEM((half, 8, 128), f32),
            VMEM((half, 2, 2, 16, stations), f32),
            dma, dma((8,)), dma((2,)), dma,
            dma((32,)), dma((32,)),
            dma((33,)), dma((33,)),
            dma((8,)), dma((8,)),
            dma((16,)), dma((16,)),
            dma((4,)), dma((4,)),
            dma((4,)), dma((4,)), dma((4,)),
        ],
        compiler_params=pltpu.CompilerParams(
            collective_id=1, has_side_effects=True, vmem_limit_bytes=60 << 20
        ),
        name="whole",
    )(coords, cells, positions, dest, directions, strip, freq, flux, index)


def hand_on_kernel(in_hbm, out_hbm, held, in_sem, out_sem):
    parts = in_sem.shape[0]
    size = in_hbm.shape[0] // parts
    slices = [slice(i * size, (i + 1) * size) for i in range(parts)]
    loads = [
        pltpu.make_async_copy(in_hbm.at[here], held.at[here], in_sem.at[i])
        for i, here in enumerate(slices)
    ]
    stores = [
        pltpu.make_async_copy(held.at[here], out_hbm.at[here], out_sem.at[i])
        for i, here in enumerate(slices)
    ]
    for load in loads:
        load.start()
    for load, store in zip(loads, stores):
        load.wait()
        store.start()
    for store in stores:
        store.wait()


def hand_on(x):
    return pl.pallas_call(
        hand_on_kernel,
        out_shape=jax.ShapeDtypeStruct(x.shape, x.dtype),
        in_specs=[pl.BlockSpec(memory_space=pl.ANY)],
        out_specs=pl.BlockSpec(memory_space=pl.ANY),
        scratch_shapes=[
            VMEM(x.shape, x.dtype),
            pltpu.SemaphoreType.DMA((8,)),
            pltpu.SemaphoreType.DMA((8,)),
        ],
        compiler_params=pltpu.CompilerParams(vmem_limit_bytes=60 << 20),
        name="hand_on",
    )(x)


def body(
    screen, pierce_coords, query_dest, positions, directions, freq_ratio, source_flux, spectral_index
):
    groups = lax.axis_size("stn")
    capacity = query_dest.shape[3]
    rows = screen.shape[0] * screen.shape[1]
    cols = screen.shape[2]
    coords = pierce_coords.reshape(2, groups, capacity)
    row_low = jnp.clip(jnp.floor(coords[0] * (rows - 1)), 0.0, rows - 2.0).astype(jnp.int32)
    col_low = jnp.clip(jnp.floor(coords[1] * (cols - 1)), 0.0, cols - 2.0).astype(jnp.int32)
    visible = whole(
        coords,
        col_low // 127 * rows + row_low,
        positions,
        query_dest.reshape(groups, capacity),
        directions,
        screen.reshape(rows, cols),
        freq_ratio,
        source_flux.reshape(-1, 128),
        spectral_index.reshape(-1, 128),
    )
    return hand_on(visible)


def solution(mesh):
    in_specs = (
        P("stn", None, None),
        P(None, "stn", "chan", None, None),
        P("stn", "chan", None, None),
        P(None, "stn"),
        P(),
        P("chan"),
        P(),
        P(),
    )
    out_specs = P("chan", None, "stn", None)
    return jax.shard_map(body, mesh=mesh, in_specs=in_specs, out_specs=out_specs, check_vma=False)
```

```python
import functools
import math

import jax
import jax.numpy as jnp
from jax import lax
from jax.experimental import pallas as pl
from jax.experimental.pallas import tpu as pltpu
from jax.sharding import PartitionSpec as P

MESH = pl.DeviceIdType.MESH
TWO_PI = 2.0 * math.pi
VMEM = pltpu.VMEM
NT = (((1,), (1,)), ((), ()))

SIN_COEFS = (4.442852586664358, -7.306899436200296, 3.59017447630795, -0.7735545907233887)
PHASE_STEPS = 34000.0


def half_turn_phasor(turns):
    r = turns - jnp.round(turns)
    u = r * r
    s = r * (SIN_COEFS[0] + u * (SIN_COEFS[1] + u * (SIN_COEFS[2] + u * SIN_COEFS[3])))
    q = s * s
    w = jnp.maximum(2.0 - q, 1e-12)
    return 1.0 - q, s * (w * lax.rsqrt(w))


LAYERS = (1, 7, 4, 3, 5, 2, 6, 0)


def wrap(value, size):
    return jnp.where(value >= size, value - size, value)


def layer_at(i):
    layer = LAYERS[-1]
    for j, other in enumerate(LAYERS[:-1]):
        layer = jnp.where(i == j, other, layer)
    return layer


def whole_kernel(
    coords_hbm, cells_hbm, positions_hbm, dest_hbm, directions_hbm, screen_hbm, freq_hbm, flux_hbm, index_hbm,
    out_hbm,
    strip, coords_ref, msg, got, addr_smem, wide, stage, sampled, back, blocks,
    positions_ref, dest_ref, directions_ref, freq_ref, flux_ref, index_ref,
    delays, delay, phase, phasor, intensity, inverse, total_ref,
    screen_sem, in_sem, addr_sem, ask_send, ask_recv, back_send, back_recv,
    z_send, z_recv, xy_send, xy_recv, core_send, core_recv, vis_send, vis_recv, own_sem,
):
    g = lax.axis_index("stn")
    c = lax.axis_index("chan")
    n = 32
    z = g // 4
    sub = g % 4
    xh = sub // 2
    core = g % 2
    sibling = g + 1 - 2 * core
    rows = strip.shape[0]
    barrier = pltpu.get_barrier_semaphore()
    y = c // 2
    xl = c % 2
    chip = [(0, 1), (1, 0), (1, 1)]
    xy = [(0, h, l) for h, l in chip]
    xy += [(dy, h, l) for dy in range(1, 4) for h, l in [(0, 0)] + chip]
    stn = [(dz, r) for dz in LAYERS for r in range(4) if (dz, r) != (0, 0)]

    def xy_peer(dy, h, l):
        return (z * 4 + wrap(xh + h, 2) * 2 + core, wrap(y + dy, 4) * 2 + wrap(xl + l, 2))

    def stn_peer(dz, r):
        return wrap(z + dz, 8) * 4 + wrap(sub + r, 4)

    screen_copy = pltpu.make_async_copy(screen_hbm, strip, screen_sem)
    coords_copy = pltpu.make_async_copy(coords_hbm, coords_ref, in_sem.at[0])
    cells_copy = pltpu.make_async_copy(cells_hbm, msg.at[0], in_sem.at[7])
    positions_copy = pltpu.make_async_copy(positions_hbm, positions_ref, in_sem.at[1])
    later = [
        pltpu.make_async_copy(source, target, in_sem.at[2 + i])
        for i, (source, target) in enumerate(
            (
                (dest_hbm, dest_ref),
                (directions_hbm, directions_ref),
                (freq_hbm, freq_ref),
                (flux_hbm, flux_ref),
                (index_hbm, index_ref),
            )
        )
    ]
    for copy in [coords_copy, cells_copy, positions_copy, screen_copy] + later:
        copy.start()
    for dz in (4, 3, 5, 2, 6, 1, 7, 0):
        for r in range(4):
            if dz or r:
                pl.semaphore_signal(
                    barrier, inc=1, device_id=(stn_peer(dz, r), c), device_id_type=MESH
                )
    for dy, h, l in xy:
        if dy or l:
            pl.semaphore_signal(barrier, inc=1, device_id=xy_peer(dy, h, l), device_id_type=MESH)
    positions_copy.wait()
    station_row = jnp.concatenate(
        [positions_ref[j : j + 1, :] for j in range(3)] + [jnp.zeros((1, 80), jnp.float32)], axis=1
    )
    msg[3] = jnp.broadcast_to((station_row * 2.0**24).astype(jnp.int32), (n, 128))
    coords_copy.wait()
    cells_copy.wait()
    cell = jnp.clip(msg[0], 0, 5 * rows - 2)
    msg[0] = cell
    low_row = (cell % rows).astype(jnp.float32)
    low_col = (cell // rows * 127).astype(jnp.float32)
    msg[1] = ((coords_ref[0] * (rows - 1) - low_row) * 2.0**24).astype(jnp.int32)
    msg[2] = ((coords_ref[1] * (strip.shape[1] - 1) - low_col) * 2.0**23).astype(jnp.int32)
    screen_copy.wait()
    step = 64

    def widen(i, carry):
        here = pl.ds(pl.multiple_of(i * step, step), step)
        lane = lax.broadcasted_iota(jnp.int32, (step, 128), 1)
        tiles = [strip[here, m * 128 : (m + 1) * 128] for m in range(4)]
        wide[here, :] = tiles[0]
        for b in range(1, 5):
            mixed = tiles[3] if b == 4 else jnp.where(lane >= 128 - b, tiles[b - 1], tiles[b])
            wide[pl.ds(pl.multiple_of(b * rows + i * step, step), step), :] = pltpu.roll(mixed, b, 1)
        return carry

    lax.fori_loop(0, rows // step, widen, 0)

    got[:, pl.ds(g, 1)] = msg[:, pl.ds(g, 1)]
    pl.semaphore_wait(barrier, n - 1 + 14)

    def ask(dz, r):
        to = wrap(z + 8 - dz, 8) * 4 + wrap(sub + r, 4)
        return pltpu.make_async_remote_copy(
            src_ref=msg.at[:, pl.ds(to, 1)],
            dst_ref=got.at[:, pl.ds(g, 1)],
            send_sem=ask_send.at[dz * 4 + r],
            recv_sem=ask_recv.at[dz * 4 + r],
            device_id=(to, c),
            device_id_type=MESH,
        )

    for dz, r in stn:
        ask(dz, r).start()
    for copy in later:
        copy.wait()

    def answer(dz, r):
        to = stn_peer(dz, r)
        return pltpu.make_async_remote_copy(
            src_ref=sampled.at[pl.ds(to, 1)],
            dst_ref=back.at[pl.ds(g, 1)],
            send_sem=back_send.at[dz * 4 + r],
            recv_sem=back_recv.at[dz * 4 + r],
            device_id=(to, c),
            device_id_type=MESH,
        )

    def cells_to_smem(dz):
        here = pl.ds(wrap(z + dz, 8) * 4, 4)
        return pltpu.make_async_copy(got.at[0, here], addr_smem.at[here], addr_sem.at[dz])

    def receive(dz):
        @pl.when(dz != 0)
        def _():
            ask(dz, 0).wait_recv()

        for r in range(1, 4):
            ask(dz, r).wait_recv()
        cells_to_smem(dz).start()

    depth = lax.broadcasted_iota(jnp.int32, (128, 128), 0).astype(jnp.float32)
    receive(LAYERS[0])

    def look_up(i, carry):
        dz = layer_at(i)

        @pl.when(i < 7)
        def _():
            receive(layer_at(i + 1))

        cells_to_smem(dz).wait()
        for r in range(4):
            to = stn_peer(dz, r)
            for j in range(128):
                stage[r, 2 * j : 2 * j + 2, :] = wide[pl.ds(addr_smem[to, j], 2), :]
            low = stage[r, pl.ds(0, 128, stride=2), :].T
            high = stage[r, pl.ds(1, 128, stride=2), :].T
            fy = got[1, pl.ds(to, 1), :].astype(jnp.float32) * 2.0**-24
            x = got[2, pl.ds(to, 1), :].astype(jnp.float32) * 2.0**-23
            mixed = (1.0 - fy) * low + fy * high
            tent = jnp.maximum(1.0 - jnp.abs(depth - x), 0.0)
            sampled[pl.ds(to, 1), :] = jnp.sum(mixed * tent, axis=0, keepdims=True)

        @pl.when(dz != 0)
        def _():
            answer(dz, 0).start()

        for r in range(1, 4):
            answer(dz, r).start()
        return carry

    lax.fori_loop(0, 8, look_up, 0)
    back[pl.ds(g, 1)] = sampled[pl.ds(g, 1)]
    for dz, r in stn:
        answer(dz, r).wait_recv()

    total = jnp.zeros((24, 128), jnp.float32)
    row_id = lax.broadcasted_iota(jnp.int32, (8, 128), 0)
    lane_id = lax.broadcasted_iota(jnp.int32, (128, 128), 0)
    for j in range(0, n, 2):
        left, right = [], []
        for o in (j, j + 1):
            v = back[o : o + 1, :]
            dest = dest_ref[o : o + 1, :]
            a = (dest // 64) % 8
            b = (dest // 512) * 64 + dest % 64
            hi = v.astype(jnp.bfloat16).astype(jnp.float32)
            mid = (v - hi).astype(jnp.bfloat16).astype(jnp.float32)
            lo = v - hi - mid
            hit = row_id == a
            left.append(
                jnp.concatenate([jnp.where(hit, part, 0.0) for part in (hi, mid, lo)], axis=0)
            )
            right.append(jnp.where(lane_id == b, 1.0, 0.0))
        total = total + lax.dot_general(
            jnp.concatenate(left, axis=1).astype(jnp.bfloat16),
            jnp.concatenate(right, axis=1).astype(jnp.bfloat16),
            NT,
            preferred_element_type=jnp.float32,
        )
    mine = jnp.round((total[0:8] + total[8:16] + total[16:24]) * (PHASE_STEPS / TWO_PI))
    mine = mine.astype(jnp.int32)
    own_rows = pl.ds(4 * z, 4)
    blocks[y, core, xh, xl, own_rows] = (mine[0:4] << 16) | (mine[4:8] & 0xFFFF)

    z_copies = []
    for k in (4, 3, 5, 2, 6, 1, 7):
        copy = pltpu.make_async_remote_copy(
            src_ref=blocks.at[y, core, xh, xl, own_rows],
            dst_ref=blocks.at[y, core, xh, xl, own_rows],
            send_sem=z_send.at[k],
            recv_sem=z_recv.at[k],
            device_id=(wrap(z + k, 8) * 4 + sub, c),
            device_id_type=MESH,
        )
        copy.start()
        z_copies.append(copy)

    turned = (got[3].astype(jnp.float32) * 2.0**-24).T
    for block in range(n):
        cols = [turned[j * 16 : (j + 1) * 16, block : block + 1] for j in range(3)]
        for m in range(4):
            lanes = slice(m * 128, (m + 1) * 128)
            delays[m, block * 16 : (block + 1) * 16, :] = (
                cols[0] * directions_ref[0:1, lanes] + cols[1] * directions_ref[1:2, lanes]
            ) + cols[2] * directions_ref[2:3, lanes]
    half = freq_ref.shape[0] // 2
    sources = flux_ref.shape[0] * 128

    def prepare(i, carry):
        freq = jnp.full((8, 128), freq_ref[core * half + i], jnp.float32)
        inverse[i] = (1.0 / PHASE_STEPS) / freq
        intensity[i] = (
            flux_ref[...]
            * jnp.exp(index_ref[...] * jnp.log(freq[0:4]))
            * (1.0 / math.sqrt(sources))
        )
        total_ref[i] = jnp.zeros(total_ref.shape[1:], jnp.float32)
        return carry

    lax.fori_loop(0, half, prepare, 0)

    for copy in z_copies:
        copy.wait_recv()

    xy_copies = {}
    for dy, h, l in xy:
        copy = pltpu.make_async_remote_copy(
            src_ref=blocks.at[y, core, xh, xl],
            dst_ref=blocks.at[y, core, xh, xl],
            send_sem=xy_send.at[dy * 4 + h * 2 + l],
            recv_sem=xy_recv.at[dy * 4 + h * 2 + l],
            device_id=xy_peer(dy, h, l),
            device_id_type=MESH,
        )
        copy.start()
        xy_copies[dy, h, l] = copy

    def to_sibling(k):
        block = blocks.at[wrap(y + 4 - k, 4), core]
        return pltpu.make_async_remote_copy(
            src_ref=block,
            dst_ref=block,
            send_sem=core_send.at[k],
            recv_sem=core_recv.at[k],
            device_id=(sibling, c),
            device_id_type=MESH,
        )

    for h, l in chip:
        xy_copies[0, h, l].wait_recv()
    to_sibling(0).start()

    lane = lax.broadcasted_iota(jnp.int32, (8, 128), 1)
    sublane = lax.broadcasted_iota(jnp.int32, (8, 128), 0)

    def spread(k):
        to_sibling(k).wait_recv()
        m = wrap(y + 4 - k, 4)
        delay[...] = delays[m]
        for pair in range(4):
            here = slice(pair * 8, (pair + 1) * 8)
            for group in range(4):
                kk, hh = group % 2, group // 2
                high, low = [], []
                for words in (blocks[m, kk, hh, 0, here], blocks[m, kk, hh, 1, here]):
                    high.append((words >> 16).astype(jnp.float32))
                    low.append(((words << 16) >> 16).astype(jnp.float32))
                for which in range(2):
                    even, odd = [
                        jnp.where(sublane < 4, hi, pltpu.roll(lo, 4, 0))
                        if which == 0
                        else jnp.where(sublane < 4, pltpu.roll(hi, 4, 0), lo)
                        for hi, lo in zip(high, low)
                    ]
                    first = ((2 * pair + which) * 4 + group) * 16
                    phase[first : first + 8] = jnp.where(lane < 64, even, pltpu.roll(odd, 64, 1))
                    phase[first + 8 : first + 16] = jnp.where(
                        lane < 64, pltpu.roll(even, 64, 1), odd
                    )

    stations = phase.shape[0]
    tile = 16
    chip_rows = pl.ds(pl.multiple_of((g // 2) * 32, 32), 32)

    def add_channels(k, first, count):
        m = wrap(y + 4 - k, 4)
        for j in range(count):
            f = first + j
            freq = freq_ref[core * half + f]
            inv = inverse[f, 0:1]

            def phasors(here):
                re, im = half_turn_phasor(freq * delay[here, :] + inv * phase[here, :])
                return re.astype(jnp.bfloat16), im.astype(jnp.bfloat16)

            re, im = phasors(chip_rows)
            weight = intensity[f, pl.ds(m, 1)]
            re = (re.astype(jnp.float32) * weight).astype(jnp.bfloat16)
            im = (im.astype(jnp.float32) * weight).astype(jnp.bfloat16)
            left = jnp.concatenate(
                [jnp.concatenate([re, im], axis=1), jnp.concatenate([im, -re], axis=1)], axis=0
            )
            for t in range(stations // tile):
                here = slice(t * tile, (t + 1) * tile)
                re, im = phasors(here)
                phasor[j, here, :128] = re
                phasor[j, here, 128:] = im
            result = lax.dot_general(left, phasor[j], NT, preferred_element_type=jnp.float32)
            total_ref[f] = total_ref[f] + result.reshape(total_ref.shape[1:])

    def send(i, count):
        here = pl.ds(i * count, count)
        there = pl.ds(core * half + i * count, count)
        return (
            pltpu.make_async_copy(total_ref.at[here, :, core], out_hbm.at[there], own_sem.at[i]),
            pltpu.make_async_remote_copy(
                src_ref=total_ref.at[here, :, 1 - core],
                dst_ref=out_hbm.at[there],
                send_sem=vis_send.at[i],
                recv_sem=vis_recv.at[i],
                device_id=(sibling, c),
                device_id_type=MESH,
            ),
        )

    def finish(i, count):
        lanes = pl.ds(pl.multiple_of((g // 8) * 128, 128), 128)
        row = lax.broadcasted_iota(jnp.int32, (2, 16, 128), 0) * 16
        row = row + lax.broadcasted_iota(jnp.int32, (2, 16, 128), 1) + ((g // 2) % 4) * 32
        cross = lax.broadcasted_iota(jnp.int32, (2, 16, 128), 2) != row
        for j in range(count):
            for part in range(2):
                block = total_ref[i * count + j, part, :, :, lanes]
                total_ref[i * count + j, part, :, :, lanes] = jnp.where(cross, block, 0.0)
        for copy in send(i, count):
            copy.start()

    batch = half // 2
    quarter = half // 4

    def chunk(i, carry):
        k = i // 2

        @pl.when(i % 2 == 0)
        def _():
            spread(k)

        add_channels(k, (i % 2) * batch, batch)

        @pl.when(i == 0)
        def _():
            for dy in range(1, 4):
                for h, l in [(0, 0)] + chip:
                    xy_copies[dy, h, l].wait_recv()
                to_sibling(dy).start()

        return carry

    lax.fori_loop(0, 7, chunk, 0)
    for i in range(2):
        finish(i, quarter)

    def last(i, carry):
        add_channels(3, i * quarter, quarter)
        finish(i, quarter)
        return carry

    lax.fori_loop(2, 4, last, 0)
    for dz, r in stn:
        ask(dz, r).wait_send()
        answer(dz, r).wait_send()
    for copy in z_copies + list(xy_copies.values()):
        copy.wait_send()
    for k in range(4):
        to_sibling(k).wait_send()
        for copy in send(k, quarter):
            copy.wait()


def whole(coords, cells, positions, dest, directions, strip, freq, flux, index):
    dma = pltpu.SemaphoreType.DMA
    n = dest.shape[0]
    rows = strip.shape[0]
    channels = freq.shape[0]
    half = channels // 2
    stations = 16 * n
    bf16, f32 = jnp.bfloat16, jnp.float32
    return pl.pallas_call(
        whole_kernel,
        out_shape=jax.ShapeDtypeStruct((channels, 2, 16, stations), f32),
        in_specs=[pl.BlockSpec(memory_space=pl.ANY)] * 9,
        out_specs=pl.BlockSpec(memory_space=pl.ANY),
        scratch_shapes=[
            VMEM(strip.shape, f32),
            VMEM((2, n, 128), f32),
            VMEM((4, n, 128), jnp.int32),
            VMEM((4, n, 128), jnp.int32),
            pltpu.SMEM((n, 128), jnp.int32),
            VMEM((5 * rows, 128), f32),
            VMEM((4, 256, 128), f32),
            VMEM((n, 128), f32),
            VMEM((n, 128), f32),
            VMEM((4, 2, 2, 2, 32, 128), jnp.int32),
            VMEM(positions.shape, f32),
            VMEM(dest.shape, jnp.int32),
            VMEM(directions.shape, f32),
            pltpu.SMEM(freq.shape, f32),
            VMEM(flux.shape, f32),
            VMEM(index.shape, f32),
            VMEM((4, stations, 128), f32),
            VMEM((stations, 128), f32),
            VMEM((stations, 128), f32),
            VMEM((half // 2, stations, 256), bf16),
            VMEM((half, 4, 128), f32),
            VMEM((half, 8, 128), f32),
            VMEM((half, 2, 2, 16, stations), f32),
            dma, dma((8,)), dma((8,)),
            dma((32,)), dma((32,)),
            dma((32,)), dma((32,)),
            dma((8,)), dma((8,)),
            dma((16,)), dma((16,)),
            dma((4,)), dma((4,)),
            dma((4,)), dma((4,)), dma((4,)),
        ],
        compiler_params=pltpu.CompilerParams(
            collective_id=1, has_side_effects=True, vmem_limit_bytes=60 << 20
        ),
        name="whole",
    )(coords, cells, positions, dest, directions, strip, freq, flux, index)


def hand_on_kernel(in_hbm, out_hbm, held, in_sem, out_sem):
    parts = in_sem.shape[0]
    size = in_hbm.shape[0] // parts
    slices = [slice(i * size, (i + 1) * size) for i in range(parts)]
    loads = [
        pltpu.make_async_copy(in_hbm.at[here], held.at[here], in_sem.at[i])
        for i, here in enumerate(slices)
    ]
    stores = [
        pltpu.make_async_copy(held.at[here], out_hbm.at[here], out_sem.at[i])
        for i, here in enumerate(slices)
    ]
    for load in loads:
        load.start()
    for load, store in zip(loads, stores):
        load.wait()
        store.start()
    for store in stores:
        store.wait()


def hand_on(x):
    return pl.pallas_call(
        hand_on_kernel,
        out_shape=jax.ShapeDtypeStruct(x.shape, x.dtype),
        in_specs=[pl.BlockSpec(memory_space=pl.ANY)],
        out_specs=pl.BlockSpec(memory_space=pl.ANY),
        scratch_shapes=[
            VMEM(x.shape, x.dtype),
            pltpu.SemaphoreType.DMA((8,)),
            pltpu.SemaphoreType.DMA((8,)),
        ],
        compiler_params=pltpu.CompilerParams(vmem_limit_bytes=60 << 20),
        name="hand_on",
    )(x)


def body(
    screen, pierce_coords, query_dest, positions, directions, freq_ratio, source_flux, spectral_index
):
    groups = lax.axis_size("stn")
    capacity = query_dest.shape[3]
    rows = screen.shape[0] * screen.shape[1]
    cols = screen.shape[2]
    coords = pierce_coords.reshape(2, groups, capacity)
    row_low = jnp.clip(jnp.floor(coords[0] * (rows - 1)), 0.0, rows - 2.0).astype(jnp.int32)
    col_low = jnp.clip(jnp.floor(coords[1] * (cols - 1)), 0.0, cols - 2.0).astype(jnp.int32)
    visible = whole(
        coords,
        col_low // 127 * rows + row_low,
        positions,
        query_dest.reshape(groups, capacity),
        directions,
        screen.reshape(rows, cols),
        freq_ratio,
        source_flux.reshape(-1, 128),
        spectral_index.reshape(-1, 128),
    )
    return hand_on(visible)


def solution(mesh):
    in_specs = (
        P("stn", None, None),
        P(None, "stn", "chan", None, None),
        P("stn", "chan", None, None),
        P(None, "stn"),
        P(),
        P("chan"),
        P(),
        P(),
    )
    out_specs = P("chan", None, "stn", None)
    return jax.shard_map(body, mesh=mesh, in_specs=in_specs, out_specs=out_specs, check_vma=False)
```

```python
import functools
import math

import jax
import jax.numpy as jnp
from jax import lax
from jax.experimental import pallas as pl
from jax.experimental.pallas import tpu as pltpu
from jax.sharding import PartitionSpec as P

MESH = pl.DeviceIdType.MESH
TWO_PI = 2.0 * math.pi
VMEM = pltpu.VMEM
NT = (((1,), (1,)), ((), ()))

SIN_COEFS = (4.442852586664358, -7.306899436200296, 3.59017447630795, -0.7735545907233887)
PHASE_STEPS = 34000.0


def half_turn_phasor(turns):
    r = turns - jnp.round(turns)
    u = r * r
    s = r * (SIN_COEFS[0] + u * (SIN_COEFS[1] + u * (SIN_COEFS[2] + u * SIN_COEFS[3])))
    q = s * s
    w = 2.000001 - q
    return 1.0 - q, s * (w * lax.rsqrt(w))


LAYERS = (1, 7, 4, 3, 5, 2, 6, 0)


def wrap(value, size):
    return jnp.where(value >= size, value - size, value)


def layer_at(i):
    layer = LAYERS[-1]
    for j, other in enumerate(LAYERS[:-1]):
        layer = jnp.where(i == j, other, layer)
    return layer


def whole_kernel(
    coords_hbm, cells_hbm, positions_hbm, dest_hbm, directions_hbm, screen_hbm, freq_hbm, flux_hbm, index_hbm,
    out_hbm,
    strip, coords_ref, msg, got, addr_smem, wide, stage, sampled, back, blocks,
    positions_ref, dest_ref, directions_ref, freq_ref, flux_ref, index_ref,
    delays, turns, phase, phasor, intensity, inverse, total_ref,
    screen_sem, in_sem, addr_sem, ask_send, ask_recv, back_send, back_recv,
    z_send, z_recv, xy_send, xy_recv, vis_send, vis_recv, own_sem,
):
    g = lax.axis_index("stn")
    c = lax.axis_index("chan")
    n = 32
    z = g // 4
    sub = g % 4
    xh = sub // 2
    core = g % 2
    sibling = g + 1 - 2 * core
    rows = strip.shape[0]
    barrier = pltpu.get_barrier_semaphore()
    y = c // 2
    xl = c % 2
    chip = [(0, 1), (1, 0), (1, 1)]
    xy = [(0, h, l) for h, l in chip]
    xy += [(dy, h, l) for dy in range(1, 4) for h, l in [(0, 0)] + chip]
    stn = [(dz, r) for dz in LAYERS for r in range(4) if (dz, r) != (0, 0)]

    def xy_peer(dy, h, l):
        return (z * 4 + wrap(xh + h, 2) * 2 + core, wrap(y + dy, 4) * 2 + wrap(xl + l, 2))

    def stn_peer(dz, r):
        return wrap(z + dz, 8) * 4 + wrap(sub + r, 4)

    screen_copy = pltpu.make_async_copy(screen_hbm, strip, screen_sem)
    coords_copy = pltpu.make_async_copy(coords_hbm, coords_ref, in_sem.at[0])
    cells_copy = pltpu.make_async_copy(cells_hbm, msg.at[0], in_sem.at[7])
    positions_copy = pltpu.make_async_copy(positions_hbm, positions_ref, in_sem.at[1])
    later = [
        pltpu.make_async_copy(source, target, in_sem.at[2 + i])
        for i, (source, target) in enumerate(
            (
                (dest_hbm, dest_ref),
                (directions_hbm, directions_ref),
                (freq_hbm, freq_ref),
                (flux_hbm, flux_ref),
                (index_hbm, index_ref),
            )
        )
    ]
    for copy in [coords_copy, cells_copy, positions_copy, screen_copy] + later:
        copy.start()
    for dz in (4, 3, 5, 2, 6, 1, 7, 0):
        for r in range(4):
            if dz or r:
                pl.semaphore_signal(
                    barrier, inc=1, device_id=(stn_peer(dz, r), c), device_id_type=MESH
                )
    for dy, h, l in xy:
        if dy or l:
            pl.semaphore_signal(barrier, inc=1, device_id=xy_peer(dy, h, l), device_id_type=MESH)
    positions_copy.wait()
    station_row = jnp.concatenate(
        [positions_ref[j : j + 1, :] for j in range(3)] + [jnp.zeros((1, 80), jnp.float32)], axis=1
    )
    msg[3] = jnp.broadcast_to((station_row * 2.0**24).astype(jnp.int32), (n, 128))
    coords_copy.wait()
    cells_copy.wait()
    cell = jnp.clip(msg[0], 0, 5 * rows - 2)
    msg[0] = cell
    low_row = (cell % rows).astype(jnp.float32)
    low_col = (cell // rows * 127).astype(jnp.float32)
    msg[1] = ((coords_ref[0] * (rows - 1) - low_row) * 2.0**24).astype(jnp.int32)
    msg[2] = ((coords_ref[1] * (strip.shape[1] - 1) - low_col) * 2.0**23).astype(jnp.int32)
    screen_copy.wait()
    step = 64

    def widen(i, carry):
        here = pl.ds(pl.multiple_of(i * step, step), step)
        lane = lax.broadcasted_iota(jnp.int32, (step, 128), 1)
        tiles = [strip[here, m * 128 : (m + 1) * 128] for m in range(4)]
        wide[here, :] = tiles[0]
        for b in range(1, 5):
            mixed = tiles[3] if b == 4 else jnp.where(lane >= 128 - b, tiles[b - 1], tiles[b])
            wide[pl.ds(pl.multiple_of(b * rows + i * step, step), step), :] = pltpu.roll(mixed, b, 1)
        return carry

    lax.fori_loop(0, rows // step, widen, 0)

    got[:, pl.ds(g, 1)] = msg[:, pl.ds(g, 1)]
    pl.semaphore_wait(barrier, n - 1 + 14)

    def ask(dz, r):
        to = wrap(z + 8 - dz, 8) * 4 + wrap(sub + r, 4)
        return pltpu.make_async_remote_copy(
            src_ref=msg.at[:, pl.ds(to, 1)],
            dst_ref=got.at[:, pl.ds(g, 1)],
            send_sem=ask_send.at[dz * 4 + r],
            recv_sem=ask_recv.at[dz * 4 + r],
            device_id=(to, c),
            device_id_type=MESH,
        )

    for dz, r in stn:
        ask(dz, r).start()
    for copy in later:
        copy.wait()

    def answer(dz, r):
        to = stn_peer(dz, r)
        return pltpu.make_async_remote_copy(
            src_ref=sampled.at[pl.ds(to, 1)],
            dst_ref=back.at[pl.ds(g, 1)],
            send_sem=back_send.at[dz * 4 + r],
            recv_sem=back_recv.at[dz * 4 + r],
            device_id=(to, c),
            device_id_type=MESH,
        )

    def cells_to_smem(dz):
        here = pl.ds(wrap(z + dz, 8) * 4, 4)
        return pltpu.make_async_copy(got.at[0, here], addr_smem.at[here], addr_sem.at[dz])

    def receive(dz):
        @pl.when(dz != 0)
        def _():
            ask(dz, 0).wait_recv()

        for r in range(1, 4):
            ask(dz, r).wait_recv()
        cells_to_smem(dz).start()

    depth = lax.broadcasted_iota(jnp.int32, (128, 128), 0).astype(jnp.float32)
    receive(LAYERS[0])

    def look_up(i, carry):
        dz = layer_at(i)

        @pl.when(i < 7)
        def _():
            receive(layer_at(i + 1))

        cells_to_smem(dz).wait()
        for r in range(4):
            to = stn_peer(dz, r)
            for j in range(128):
                stage[r, 2 * j : 2 * j + 2, :] = wide[pl.ds(addr_smem[to, j], 2), :]
            low = stage[r, pl.ds(0, 128, stride=2), :].T
            high = stage[r, pl.ds(1, 128, stride=2), :].T
            fy = got[1, pl.ds(to, 1), :].astype(jnp.float32) * 2.0**-24
            x = got[2, pl.ds(to, 1), :].astype(jnp.float32) * 2.0**-23
            mixed = (1.0 - fy) * low + fy * high
            tent = jnp.maximum(1.0 - jnp.abs(depth - x), 0.0)
            sampled[pl.ds(to, 1), :] = jnp.sum(mixed * tent, axis=0, keepdims=True)

        @pl.when(dz != 0)
        def _():
            answer(dz, 0).start()

        for r in range(1, 4):
            answer(dz, r).start()
        return carry

    lax.fori_loop(0, 8, look_up, 0)
    back[pl.ds(g, 1)] = sampled[pl.ds(g, 1)]
    for dz, r in stn:
        answer(dz, r).wait_recv()

    total = jnp.zeros((24, 128), jnp.float32)
    row_id = lax.broadcasted_iota(jnp.int32, (8, 128), 0)
    lane_id = lax.broadcasted_iota(jnp.int32, (128, 128), 0)
    for j in range(0, n, 2):
        left, right = [], []
        for o in (j, j + 1):
            v = back[o : o + 1, :]
            dest = dest_ref[o : o + 1, :]
            a = (dest // 64) % 8
            b = (dest // 512) * 64 + dest % 64
            hi = v.astype(jnp.bfloat16).astype(jnp.float32)
            mid = (v - hi).astype(jnp.bfloat16).astype(jnp.float32)
            lo = v - hi - mid
            hit = row_id == a
            left.append(
                jnp.concatenate([jnp.where(hit, part, 0.0) for part in (hi, mid, lo)], axis=0)
            )
            right.append(jnp.where(lane_id == b, 1.0, 0.0))
        total = total + lax.dot_general(
            jnp.concatenate(left, axis=1).astype(jnp.bfloat16),
            jnp.concatenate(right, axis=1).astype(jnp.bfloat16),
            NT,
            preferred_element_type=jnp.float32,
        )
    mine = jnp.round((total[0:8] + total[8:16] + total[16:24]) * (PHASE_STEPS / TWO_PI))
    mine = mine.astype(jnp.int32)
    own_rows = pl.ds(4 * z, 4)
    own_words = blocks.at[y, xh, xl, core, own_rows]
    own_words[...] = (mine[0:4] << 16) | (mine[4:8] & 0xFFFF)

    z_copies = []
    for k in (4, 3, 5, 2, 6, 1, 7, 0):
        for other in range(2):
            if k or other:
                copy = pltpu.make_async_remote_copy(
                    src_ref=own_words,
                    dst_ref=own_words,
                    send_sem=z_send.at[k * 2 + other],
                    recv_sem=z_recv.at[k * 2 + other],
                    device_id=(wrap(z + k, 8) * 4 + (sub + 1 - 2 * core if other else sub), c),
                    device_id_type=MESH,
                )
                copy.start()
                z_copies.append(copy)

    turned = (got[3].astype(jnp.float32) * 2.0**-24).T
    for block in range(n):
        cols = [turned[j * 16 : (j + 1) * 16, block : block + 1] for j in range(3)]
        for m in range(4):
            lanes = slice(m * 128, (m + 1) * 128)
            delays[m, block * 16 : (block + 1) * 16, :] = (
                cols[0] * directions_ref[0:1, lanes] + cols[1] * directions_ref[1:2, lanes]
            ) + cols[2] * directions_ref[2:3, lanes]
    half = freq_ref.shape[0] // 2
    sources = flux_ref.shape[0] * 128

    def prepare(i, carry):
        freq = freq_ref[core * half + i]
        turns[i] = freq * delays[...]
        freq = jnp.full((8, 128), freq, jnp.float32)
        inverse[i] = (1.0 / PHASE_STEPS) / freq
        intensity[i] = (
            flux_ref[...]
            * jnp.exp(index_ref[...] * jnp.log(freq[0:4]))
            * (1.0 / math.sqrt(sources))
        )
        total_ref[i] = jnp.zeros(total_ref.shape[1:], jnp.float32)
        return carry

    lax.fori_loop(0, half, prepare, 0)

    for copy in z_copies:
        copy.wait_recv()

    def pass_on(dy, h, l):
        block = blocks.at[y, xh, xl]
        return pltpu.make_async_remote_copy(
            src_ref=block,
            dst_ref=block,
            send_sem=xy_send.at[dy * 4 + h * 2 + l],
            recv_sem=xy_recv.at[dy * 4 + h * 2 + l],
            device_id=xy_peer(dy, h, l),
            device_id_type=MESH,
        )

    for dy, h, l in xy:
        pass_on(dy, h, l).start()

    lane = lax.broadcasted_iota(jnp.int32, (8, 128), 1)
    sublane = lax.broadcasted_iota(jnp.int32, (8, 128), 0)

    def spread(k):
        @pl.when(k > 0)
        def _():
            pass_on(k, 0, 0).wait_recv()

        for h, l in chip:
            pass_on(k, h, l).wait_recv()
        m = wrap(y + 4 - k, 4)
        for pair in range(4):
            here = slice(pair * 8, (pair + 1) * 8)
            for group in range(4):
                kk, hh = group % 2, group // 2
                high, low = [], []
                for words in (blocks[m, hh, 0, kk, here], blocks[m, hh, 1, kk, here]):
                    high.append((words >> 16).astype(jnp.float32))
                    low.append(((words << 16) >> 16).astype(jnp.float32))
                for which in range(2):
                    even, odd = [
                        jnp.where(sublane < 4, hi, pltpu.roll(lo, 4, 0))
                        if which == 0
                        else jnp.where(sublane < 4, pltpu.roll(hi, 4, 0), lo)
                        for hi, lo in zip(high, low)
                    ]
                    first = ((2 * pair + which) * 4 + group) * 16
                    phase[first : first + 8] = jnp.where(lane < 64, even, pltpu.roll(odd, 64, 1))
                    phase[first + 8 : first + 16] = jnp.where(
                        lane < 64, pltpu.roll(even, 64, 1), odd
                    )

    stations = phase.shape[0]
    tile = 16
    chip_rows = pl.ds(pl.multiple_of((g // 2) * 32, 32), 32)

    def add_channels(k, first, count):
        m = wrap(y + 4 - k, 4)
        for j in range(count):
            f = first + j
            inv = inverse[f, 0:1]

            def phasors(here):
                re, im = half_turn_phasor(turns[f, m, here, :] + inv * phase[here, :])
                return re.astype(jnp.bfloat16), im.astype(jnp.bfloat16)

            re, im = phasors(chip_rows)
            weight = intensity[f, pl.ds(m, 1)]
            re = (re.astype(jnp.float32) * weight).astype(jnp.bfloat16)
            im = (im.astype(jnp.float32) * weight).astype(jnp.bfloat16)
            left = jnp.concatenate(
                [jnp.concatenate([re, im], axis=1), jnp.concatenate([im, -re], axis=1)], axis=0
            )
            for t in range(stations // tile):
                here = slice(t * tile, (t + 1) * tile)
                re, im = phasors(here)
                phasor[j, here, :128] = re
                phasor[j, here, 128:] = im
            result = lax.dot_general(left, phasor[j], NT, preferred_element_type=jnp.float32)
            total_ref[f] = total_ref[f] + result.reshape(total_ref.shape[1:])

    def send(i, count):
        here = pl.ds(i * count, count)
        there = pl.ds(core * half + i * count, count)
        return (
            pltpu.make_async_copy(total_ref.at[here, :, core], out_hbm.at[there], own_sem.at[i]),
            pltpu.make_async_remote_copy(
                src_ref=total_ref.at[here, :, 1 - core],
                dst_ref=out_hbm.at[there],
                send_sem=vis_send.at[i],
                recv_sem=vis_recv.at[i],
                device_id=(sibling, c),
                device_id_type=MESH,
            ),
        )

    def finish(i, count):
        lanes = pl.ds(pl.multiple_of((g // 8) * 128, 128), 128)
        row = lax.broadcasted_iota(jnp.int32, (2, 16, 128), 0) * 16
        row = row + lax.broadcasted_iota(jnp.int32, (2, 16, 128), 1) + ((g // 2) % 4) * 32
        cross = lax.broadcasted_iota(jnp.int32, (2, 16, 128), 2) != row
        for j in range(count):
            for part in range(2):
                block = total_ref[i * count + j, part, :, :, lanes]
                total_ref[i * count + j, part, :, :, lanes] = jnp.where(cross, block, 0.0)
        for copy in send(i, count):
            copy.start()

    quarter = half // 4

    def chunk(k, carry):
        spread(k)
        add_channels(k, 0, half)
        return carry

    lax.fori_loop(0, 3, chunk, 0)
    spread(3)

    def last(i, carry):
        add_channels(3, i * quarter, quarter)
        finish(i, quarter)
        return carry

    lax.fori_loop(0, 4, last, 0)
    for dz, r in stn:
        ask(dz, r).wait_send()
        answer(dz, r).wait_send()
    for copy in z_copies:
        copy.wait_send()
    for dy, h, l in xy:
        pass_on(dy, h, l).wait_send()
    for k in range(4):
        for copy in send(k, quarter):
            copy.wait()


def whole(coords, cells, positions, dest, directions, strip, freq, flux, index):
    dma = pltpu.SemaphoreType.DMA
    n = dest.shape[0]
    rows = strip.shape[0]
    channels = freq.shape[0]
    half = channels // 2
    stations = 16 * n
    bf16, f32 = jnp.bfloat16, jnp.float32
    return pl.pallas_call(
        whole_kernel,
        out_shape=jax.ShapeDtypeStruct((channels, 2, 16, stations), f32),
        in_specs=[pl.BlockSpec(memory_space=pl.ANY)] * 9,
        out_specs=pl.BlockSpec(memory_space=pl.ANY),
        scratch_shapes=[
            VMEM(strip.shape, f32),
            VMEM((2, n, 128), f32),
            VMEM((4, n, 128), jnp.int32),
            VMEM((4, n, 128), jnp.int32),
            pltpu.SMEM((n, 128), jnp.int32),
            VMEM((5 * rows, 128), f32),
            VMEM((4, 256, 128), f32),
            VMEM((n, 128), f32),
            VMEM((n, 128), f32),
            VMEM((4, 2, 2, 2, 32, 128), jnp.int32),
            VMEM(positions.shape, f32),
            VMEM(dest.shape, jnp.int32),
            VMEM(directions.shape, f32),
            pltpu.SMEM(freq.shape, f32),
            VMEM(flux.shape, f32),
            VMEM(index.shape, f32),
            VMEM((4, stations, 128), f32),
            VMEM((half, 4, stations, 128), f32),
            VMEM((stations, 128), f32),
            VMEM((half, stations, 256), bf16),
            VMEM((half, 4, 128), f32),
            VMEM((half, 8, 128), f32),
            VMEM((half, 2, 2, 16, stations), f32),
            dma, dma((8,)), dma((8,)),
            dma((32,)), dma((32,)),
            dma((32,)), dma((32,)),
            dma((16,)), dma((16,)),
            dma((16,)), dma((16,)),
            dma((4,)), dma((4,)), dma((4,)),
        ],
        compiler_params=pltpu.CompilerParams(
            collective_id=1, has_side_effects=True, vmem_limit_bytes=60 << 20
        ),
        name="whole",
    )(coords, cells, positions, dest, directions, strip, freq, flux, index)


def hand_on_kernel(in_hbm, out_hbm, held, in_sem, out_sem):
    parts = in_sem.shape[0]
    size = in_hbm.shape[0] // parts
    slices = [slice(i * size, (i + 1) * size) for i in range(parts)]
    loads = [
        pltpu.make_async_copy(in_hbm.at[here], held.at[here], in_sem.at[i])
        for i, here in enumerate(slices)
    ]
    stores = [
        pltpu.make_async_copy(held.at[here], out_hbm.at[here], out_sem.at[i])
        for i, here in enumerate(slices)
    ]
    for load in loads:
        load.start()
    for load, store in zip(loads, stores):
        load.wait()
        store.start()
    for store in stores:
        store.wait()


def hand_on(x):
    return pl.pallas_call(
        hand_on_kernel,
        out_shape=jax.ShapeDtypeStruct(x.shape, x.dtype),
        in_specs=[pl.BlockSpec(memory_space=pl.ANY)],
        out_specs=pl.BlockSpec(memory_space=pl.ANY),
        scratch_shapes=[
            VMEM(x.shape, x.dtype),
            pltpu.SemaphoreType.DMA((8,)),
            pltpu.SemaphoreType.DMA((8,)),
        ],
        compiler_params=pltpu.CompilerParams(vmem_limit_bytes=60 << 20),
        name="hand_on",
    )(x)


def body(
    screen, pierce_coords, query_dest, positions, directions, freq_ratio, source_flux, spectral_index
):
    groups = lax.axis_size("stn")
    capacity = query_dest.shape[3]
    rows = screen.shape[0] * screen.shape[1]
    cols = screen.shape[2]
    coords = pierce_coords.reshape(2, groups, capacity)
    row_low = jnp.clip(jnp.floor(coords[0] * (rows - 1)), 0.0, rows - 2.0).astype(jnp.int32)
    col_low = jnp.clip(jnp.floor(coords[1] * (cols - 1)), 0.0, cols - 2.0).astype(jnp.int32)
    visible = whole(
        coords,
        col_low // 127 * rows + row_low,
        positions,
        query_dest.reshape(groups, capacity),
        directions,
        screen.reshape(rows, cols),
        freq_ratio,
        source_flux.reshape(-1, 128),
        spectral_index.reshape(-1, 128),
    )
    return hand_on(visible)


def solution(mesh):
    in_specs = (
        P("stn", None, None),
        P(None, "stn", "chan", None, None),
        P("stn", "chan", None, None),
        P(None, "stn"),
        P(),
        P("chan"),
        P(),
        P(),
    )
    out_specs = P("chan", None, "stn", None)
    return jax.shard_map(body, mesh=mesh, in_specs=in_specs, out_specs=out_specs, check_vma=False)
```

```python
import functools
import math

import jax
import jax.numpy as jnp
from jax import lax
from jax.experimental import pallas as pl
from jax.experimental.pallas import tpu as pltpu
from jax.sharding import PartitionSpec as P

MESH = pl.DeviceIdType.MESH
TWO_PI = 2.0 * math.pi
VMEM = pltpu.VMEM
NT = (((1,), (1,)), ((), ()))

SIN_COEFS = (4.442852586664358, -7.306899436200296, 3.59017447630795, -0.7735545907233887)
PHASE_STEPS = 34000.0


def half_turn_phasor(turns):
    r = turns - jnp.round(turns)
    u = r * r
    s = r * (SIN_COEFS[0] + u * (SIN_COEFS[1] + u * (SIN_COEFS[2] + u * SIN_COEFS[3])))
    q = s * s
    w = 2.000001 - q
    return 1.0 - q, s * (w * lax.rsqrt(w))


LAYERS = (1, 7, 4, 3, 5, 2, 6, 0)


def wrap(value, size):
    return jnp.where(value >= size, value - size, value)


def layer_at(i):
    layer = LAYERS[-1]
    for j, other in enumerate(LAYERS[:-1]):
        layer = jnp.where(i == j, other, layer)
    return layer


def whole_kernel(
    coords_hbm, positions_hbm, dest_hbm, directions_hbm, screen_hbm, freq_hbm, flux_hbm, index_hbm,
    out_hbm,
    strip, coords_ref, msg, got, addr_smem, wide, stage, sampled, back, blocks,
    positions_ref, dest_ref, directions_ref, freq_ref, flux_ref, index_ref,
    delays, turns, phase, phasor, intensity, inverse, total_ref,
    screen_sem, in_sem, addr_sem, ask_send, ask_recv, back_send, back_recv,
    z_send, z_recv, xy_send, xy_recv, vis_send, vis_recv, own_sem,
):
    g = lax.axis_index("stn")
    c = lax.axis_index("chan")
    n = 32
    z = g // 4
    sub = g % 4
    xh = sub // 2
    core = g % 2
    sibling = g + 1 - 2 * core
    rows = strip.shape[0]
    barrier = pltpu.get_barrier_semaphore()
    y = c // 2
    xl = c % 2
    chip = [(0, 1), (1, 0), (1, 1)]
    xy = [(0, h, l) for h, l in chip]
    xy += [(dy, h, l) for dy in range(1, 4) for h, l in [(0, 0)] + chip]
    stn = [(dz, r) for dz in LAYERS for r in range(4) if (dz, r) != (0, 0)]

    def xy_peer(dy, h, l):
        return (z * 4 + wrap(xh + h, 2) * 2 + core, wrap(y + dy, 4) * 2 + wrap(xl + l, 2))

    def stn_peer(dz, r):
        return wrap(z + dz, 8) * 4 + wrap(sub + r, 4)

    screen_copy = pltpu.make_async_copy(screen_hbm, strip, screen_sem)
    coords_copy = pltpu.make_async_copy(coords_hbm, coords_ref, in_sem.at[0])
    positions_copy = pltpu.make_async_copy(positions_hbm, positions_ref, in_sem.at[1])
    later = [
        pltpu.make_async_copy(source, target, in_sem.at[2 + i])
        for i, (source, target) in enumerate(
            (
                (dest_hbm, dest_ref),
                (directions_hbm, directions_ref),
                (freq_hbm, freq_ref),
                (flux_hbm, flux_ref),
                (index_hbm, index_ref),
            )
        )
    ]
    for copy in [coords_copy, positions_copy, screen_copy] + later:
        copy.start()
    for dz in (4, 3, 5, 2, 6, 1, 7, 0):
        for r in range(4):
            if dz or r:
                pl.semaphore_signal(
                    barrier, inc=1, device_id=(stn_peer(dz, r), c), device_id_type=MESH
                )
    for dy, h, l in xy:
        if dy or l:
            pl.semaphore_signal(barrier, inc=1, device_id=xy_peer(dy, h, l), device_id_type=MESH)
    positions_copy.wait()
    station_row = jnp.concatenate(
        [positions_ref[j : j + 1, :] for j in range(3)] + [jnp.zeros((1, 80), jnp.float32)], axis=1
    )
    msg[3] = jnp.broadcast_to((station_row * 2.0**24).astype(jnp.int32), (n, 128))
    coords_copy.wait()
    row_pos = coords_ref[0] * (rows - 1)
    col_pos = coords_ref[1] * (strip.shape[1] - 1)
    row_low = jnp.clip(jnp.floor(row_pos), 0.0, rows - 2.0)
    col_low = jnp.clip(jnp.floor(col_pos), 0.0, strip.shape[1] - 2.0)
    column = col_low.astype(jnp.int32)
    part = column // 127
    msg[0] = jnp.clip(part * rows + row_low.astype(jnp.int32), 0, 5 * rows - 2)
    msg[1] = ((row_pos - row_low) * 2.0**24).astype(jnp.int32)
    msg[2] = ((col_pos - (part * 127).astype(jnp.float32)) * 2.0**23).astype(jnp.int32)
    screen_copy.wait()
    step = 64

    def widen(i, carry):
        here = pl.ds(pl.multiple_of(i * step, step), step)
        lane = lax.broadcasted_iota(jnp.int32, (step, 128), 1)
        tiles = [strip[here, m * 128 : (m + 1) * 128] for m in range(4)]
        wide[here, :] = tiles[0]
        for b in range(1, 5):
            mixed = tiles[3] if b == 4 else jnp.where(lane >= 128 - b, tiles[b - 1], tiles[b])
            wide[pl.ds(pl.multiple_of(b * rows + i * step, step), step), :] = pltpu.roll(mixed, b, 1)
        return carry

    lax.fori_loop(0, rows // step, widen, 0)

    got[:, pl.ds(g, 1)] = msg[:, pl.ds(g, 1)]
    pl.semaphore_wait(barrier, n - 1 + 14)

    def ask(dz, r):
        to = wrap(z + 8 - dz, 8) * 4 + wrap(sub + r, 4)
        return pltpu.make_async_remote_copy(
            src_ref=msg.at[:, pl.ds(to, 1)],
            dst_ref=got.at[:, pl.ds(g, 1)],
            send_sem=ask_send.at[dz * 4 + r],
            recv_sem=ask_recv.at[dz * 4 + r],
            device_id=(to, c),
            device_id_type=MESH,
        )

    for dz, r in stn:
        ask(dz, r).start()
    for copy in later:
        copy.wait()

    def answer(dz, r):
        to = stn_peer(dz, r)
        return pltpu.make_async_remote_copy(
            src_ref=sampled.at[pl.ds(to, 1)],
            dst_ref=back.at[pl.ds(g, 1)],
            send_sem=back_send.at[dz * 4 + r],
            recv_sem=back_recv.at[dz * 4 + r],
            device_id=(to, c),
            device_id_type=MESH,
        )

    def cells_to_smem(dz):
        here = pl.ds(wrap(z + dz, 8) * 4, 4)
        return pltpu.make_async_copy(got.at[0, here], addr_smem.at[here], addr_sem.at[dz])

    def receive(dz):
        @pl.when(dz != 0)
        def _():
            ask(dz, 0).wait_recv()

        for r in range(1, 4):
            ask(dz, r).wait_recv()
        cells_to_smem(dz).start()

    depth = lax.broadcasted_iota(jnp.int32, (128, 128), 0).astype(jnp.float32)
    receive(LAYERS[0])

    def look_up(i, carry):
        dz = layer_at(i)

        @pl.when(i < 7)
        def _():
            receive(layer_at(i + 1))

        cells_to_smem(dz).wait()
        for r in range(4):
            to = stn_peer(dz, r)
            for j in range(128):
                stage[r, 2 * j : 2 * j + 2, :] = wide[pl.ds(addr_smem[to, j], 2), :]
            low = stage[r, pl.ds(0, 128, stride=2), :].T
            high = stage[r, pl.ds(1, 128, stride=2), :].T
            fy = got[1, pl.ds(to, 1), :].astype(jnp.float32) * 2.0**-24
            x = got[2, pl.ds(to, 1), :].astype(jnp.float32) * 2.0**-23
            mixed = (1.0 - fy) * low + fy * high
            tent = jnp.maximum(1.0 - jnp.abs(depth - x), 0.0)
            sampled[pl.ds(to, 1), :] = jnp.sum(mixed * tent, axis=0, keepdims=True)

        @pl.when(dz != 0)
        def _():
            answer(dz, 0).start()

        for r in range(1, 4):
            answer(dz, r).start()
        return carry

    lax.fori_loop(0, 8, look_up, 0)
    back[pl.ds(g, 1)] = sampled[pl.ds(g, 1)]
    for dz, r in stn:
        answer(dz, r).wait_recv()

    total = jnp.zeros((24, 128), jnp.float32)
    row_id = lax.broadcasted_iota(jnp.int32, (8, 128), 0)
    lane_id = lax.broadcasted_iota(jnp.int32, (128, 128), 0)
    for j in range(0, n, 2):
        left, right = [], []
        for o in (j, j + 1):
            v = back[o : o + 1, :]
            dest = dest_ref[o : o + 1, :]
            a = (dest // 64) % 8
            b = (dest // 512) * 64 + dest % 64
            hi = v.astype(jnp.bfloat16).astype(jnp.float32)
            mid = (v - hi).astype(jnp.bfloat16).astype(jnp.float32)
            lo = v - hi - mid
            hit = row_id == a
            left.append(
                jnp.concatenate([jnp.where(hit, part, 0.0) for part in (hi, mid, lo)], axis=0)
            )
            right.append(jnp.where(lane_id == b, 1.0, 0.0))
        total = total + lax.dot_general(
            jnp.concatenate(left, axis=1).astype(jnp.bfloat16),
            jnp.concatenate(right, axis=1).astype(jnp.bfloat16),
            NT,
            preferred_element_type=jnp.float32,
        )
    mine = jnp.round((total[0:8] + total[8:16] + total[16:24]) * (PHASE_STEPS / TWO_PI))
    mine = mine.astype(jnp.int32)
    own_rows = pl.ds(4 * z, 4)
    own_words = blocks.at[y, xh, xl, core, own_rows]
    own_words[...] = (mine[0:4] << 16) | (mine[4:8] & 0xFFFF)

    z_copies = []
    for k in (4, 3, 5, 2, 6, 1, 7, 0):
        for other in range(2):
            if k or other:
                copy = pltpu.make_async_remote_copy(
                    src_ref=own_words,
                    dst_ref=own_words,
                    send_sem=z_send.at[k * 2 + other],
                    recv_sem=z_recv.at[k * 2 + other],
                    device_id=(wrap(z + k, 8) * 4 + (sub + 1 - 2 * core if other else sub), c),
                    device_id_type=MESH,
                )
                copy.start()
                z_copies.append(copy)

    turned = (got[3].astype(jnp.float32) * 2.0**-24).T
    for block in range(n):
        cols = [turned[j * 16 : (j + 1) * 16, block : block + 1] for j in range(3)]
        for m in range(4):
            lanes = slice(m * 128, (m + 1) * 128)
            delays[m, block * 16 : (block + 1) * 16, :] = (
                cols[0] * directions_ref[0:1, lanes] + cols[1] * directions_ref[1:2, lanes]
            ) + cols[2] * directions_ref[2:3, lanes]
    half = freq_ref.shape[0] // 2
    sources = flux_ref.shape[0] * 128

    def prepare(i, carry):
        freq = freq_ref[core * half + i]
        turns[i] = freq * delays[...]
        freq = jnp.full((8, 128), freq, jnp.float32)
        inverse[i] = (1.0 / PHASE_STEPS) / freq
        intensity[i] = (
            flux_ref[...]
            * jnp.exp(index_ref[...] * jnp.log(freq[0:4]))
            * (1.0 / math.sqrt(sources))
        )
        total_ref[i] = jnp.zeros(total_ref.shape[1:], jnp.float32)
        return carry

    lax.fori_loop(0, half // 2, prepare, 0)

    for copy in z_copies:
        copy.wait_recv()

    def pass_on(dy, h, l):
        block = blocks.at[y, xh, xl]
        return pltpu.make_async_remote_copy(
            src_ref=block,
            dst_ref=block,
            send_sem=xy_send.at[dy * 4 + h * 2 + l],
            recv_sem=xy_recv.at[dy * 4 + h * 2 + l],
            device_id=xy_peer(dy, h, l),
            device_id_type=MESH,
        )

    for dy, h, l in xy:
        pass_on(dy, h, l).start()
    lax.fori_loop(half // 2, half, prepare, 0)

    lane = lax.broadcasted_iota(jnp.int32, (8, 128), 1)
    sublane = lax.broadcasted_iota(jnp.int32, (8, 128), 0)

    def spread(k):
        @pl.when(k > 0)
        def _():
            pass_on(k, 0, 0).wait_recv()

        for h, l in chip:
            pass_on(k, h, l).wait_recv()
        m = wrap(y + 4 - k, 4)
        for pair in range(4):
            here = slice(pair * 8, (pair + 1) * 8)
            for group in range(4):
                kk, hh = group % 2, group // 2
                high, low = [], []
                for words in (blocks[m, hh, 0, kk, here], blocks[m, hh, 1, kk, here]):
                    high.append((words >> 16).astype(jnp.float32))
                    low.append(((words << 16) >> 16).astype(jnp.float32))
                for which in range(2):
                    even, odd = [
                        jnp.where(sublane < 4, hi, pltpu.roll(lo, 4, 0))
                        if which == 0
                        else jnp.where(sublane < 4, pltpu.roll(hi, 4, 0), lo)
                        for hi, lo in zip(high, low)
                    ]
                    first = ((2 * pair + which) * 4 + group) * 16
                    phase[first : first + 8] = jnp.where(lane < 64, even, pltpu.roll(odd, 64, 1))
                    phase[first + 8 : first + 16] = jnp.where(
                        lane < 64, pltpu.roll(even, 64, 1), odd
                    )

    stations = phase.shape[0]
    tile = 16
    chip_rows = pl.ds(pl.multiple_of((g // 2) * 32, 32), 32)

    def add_channels(k, first, count):
        m = wrap(y + 4 - k, 4)
        for j in range(count):
            f = first + j
            inv = inverse[f, 0:1]

            def phasors(here):
                re, im = half_turn_phasor(turns[f, m, here, :] + inv * phase[here, :])
                return re.astype(jnp.bfloat16), im.astype(jnp.bfloat16)

            re, im = phasors(chip_rows)
            weight = intensity[f, pl.ds(m, 1)]
            re = (re.astype(jnp.float32) * weight).astype(jnp.bfloat16)
            im = (im.astype(jnp.float32) * weight).astype(jnp.bfloat16)
            left = jnp.concatenate(
                [jnp.concatenate([re, im], axis=1), jnp.concatenate([im, -re], axis=1)], axis=0
            )
            for t in range(stations // tile):
                here = slice(t * tile, (t + 1) * tile)
                re, im = phasors(here)
                phasor[j, here, :128] = re
                phasor[j, here, 128:] = im
            result = lax.dot_general(left, phasor[j], NT, preferred_element_type=jnp.float32)
            total_ref[f] = total_ref[f] + result.reshape(total_ref.shape[1:])

    def send(i, count):
        here = pl.ds(i * count, count)
        there = pl.ds(core * half + i * count, count)
        return (
            pltpu.make_async_copy(total_ref.at[here, :, core], out_hbm.at[there], own_sem.at[i]),
            pltpu.make_async_remote_copy(
                src_ref=total_ref.at[here, :, 1 - core],
                dst_ref=out_hbm.at[there],
                send_sem=vis_send.at[i],
                recv_sem=vis_recv.at[i],
                device_id=(sibling, c),
                device_id_type=MESH,
            ),
        )

    def finish(i, count):
        lanes = pl.ds(pl.multiple_of((g // 8) * 128, 128), 128)
        row = lax.broadcasted_iota(jnp.int32, (2, 16, 128), 0) * 16
        row = row + lax.broadcasted_iota(jnp.int32, (2, 16, 128), 1) + ((g // 2) % 4) * 32
        cross = lax.broadcasted_iota(jnp.int32, (2, 16, 128), 2) != row
        for j in range(count):
            for part in range(2):
                block = total_ref[i * count + j, part, :, :, lanes]
                total_ref[i * count + j, part, :, :, lanes] = jnp.where(cross, block, 0.0)
        for copy in send(i, count):
            copy.start()

    quarter = half // 4

    def chunk(k, carry):
        spread(k)
        add_channels(k, 0, half)
        return carry

    lax.fori_loop(0, 3, chunk, 0)
    spread(3)

    def last(i, carry):
        add_channels(3, i * quarter, quarter)
        finish(i, quarter)
        return carry

    lax.fori_loop(0, 4, last, 0)
    for dz, r in stn:
        ask(dz, r).wait_send()
        answer(dz, r).wait_send()
    for copy in z_copies:
        copy.wait_send()
    for dy, h, l in xy:
        pass_on(dy, h, l).wait_send()
    for k in range(4):
        for copy in send(k, quarter):
            copy.wait()


def whole(coords, positions, dest, directions, strip, freq, flux, index):
    dma = pltpu.SemaphoreType.DMA
    n = dest.shape[0]
    rows = strip.shape[0]
    channels = freq.shape[0]
    half = channels // 2
    stations = 16 * n
    bf16, f32 = jnp.bfloat16, jnp.float32
    return pl.pallas_call(
        whole_kernel,
        out_shape=jax.ShapeDtypeStruct((channels, 2, 16, stations), f32),
        in_specs=[pl.BlockSpec(memory_space=pl.ANY)] * 8,
        out_specs=pl.BlockSpec(memory_space=pl.ANY),
        scratch_shapes=[
            VMEM(strip.shape, f32),
            VMEM((2, n, 128), f32),
            VMEM((4, n, 128), jnp.int32),
            VMEM((4, n, 128), jnp.int32),
            pltpu.SMEM((n, 128), jnp.int32),
            VMEM((5 * rows, 128), f32),
            VMEM((4, 256, 128), f32),
            VMEM((n, 128), f32),
            VMEM((n, 128), f32),
            VMEM((4, 2, 2, 2, 32, 128), jnp.int32),
            VMEM(positions.shape, f32),
            VMEM(dest.shape, jnp.int32),
            VMEM(directions.shape, f32),
            pltpu.SMEM(freq.shape, f32),
            VMEM(flux.shape, f32),
            VMEM(index.shape, f32),
            VMEM((4, stations, 128), f32),
            VMEM((half, 4, stations, 128), f32),
            VMEM((stations, 128), f32),
            VMEM((half, stations, 256), bf16),
            VMEM((half, 4, 128), f32),
            VMEM((half, 8, 128), f32),
            VMEM((half, 2, 2, 16, stations), f32),
            dma, dma((8,)), dma((8,)),
            dma((32,)), dma((32,)),
            dma((32,)), dma((32,)),
            dma((16,)), dma((16,)),
            dma((16,)), dma((16,)),
            dma((4,)), dma((4,)), dma((4,)),
        ],
        compiler_params=pltpu.CompilerParams(
            collective_id=1, has_side_effects=True, vmem_limit_bytes=60 << 20
        ),
        name="whole",
    )(coords, positions, dest, directions, strip, freq, flux, index)


def hand_on_kernel(in_hbm, out_hbm, held, in_sem, out_sem):
    parts = in_sem.shape[0]
    size = in_hbm.shape[0] // parts
    slices = [slice(i * size, (i + 1) * size) for i in range(parts)]
    loads = [
        pltpu.make_async_copy(in_hbm.at[here], held.at[here], in_sem.at[i])
        for i, here in enumerate(slices)
    ]
    stores = [
        pltpu.make_async_copy(held.at[here], out_hbm.at[here], out_sem.at[i])
        for i, here in enumerate(slices)
    ]
    for load in loads:
        load.start()
    for load, store in zip(loads, stores):
        load.wait()
        store.start()
    for store in stores:
        store.wait()


def hand_on(x):
    return pl.pallas_call(
        hand_on_kernel,
        out_shape=jax.ShapeDtypeStruct(x.shape, x.dtype),
        in_specs=[pl.BlockSpec(memory_space=pl.ANY)],
        out_specs=pl.BlockSpec(memory_space=pl.ANY),
        scratch_shapes=[
            VMEM(x.shape, x.dtype),
            pltpu.SemaphoreType.DMA((4,)),
            pltpu.SemaphoreType.DMA((4,)),
        ],
        compiler_params=pltpu.CompilerParams(vmem_limit_bytes=60 << 20),
        name="hand_on",
    )(x)


def body(
    screen, pierce_coords, query_dest, positions, directions, freq_ratio, source_flux, spectral_index
):
    groups = lax.axis_size("stn")
    capacity = query_dest.shape[3]
    rows = screen.shape[0] * screen.shape[1]
    cols = screen.shape[2]
    coords = pierce_coords.reshape(2, groups, capacity)
    visible = whole(
        coords,
        positions,
        query_dest.reshape(groups, capacity),
        directions,
        screen.reshape(rows, cols),
        freq_ratio,
        source_flux.reshape(-1, 128),
        spectral_index.reshape(-1, 128),
    )
    return hand_on(visible)


def solution(mesh):
    in_specs = (
        P("stn", None, None),
        P(None, "stn", "chan", None, None),
        P("stn", "chan", None, None),
        P(None, "stn"),
        P(),
        P("chan"),
        P(),
        P(),
    )
    out_specs = P("chan", None, "stn", None)
    return jax.shard_map(body, mesh=mesh, in_specs=in_specs, out_specs=out_specs, check_vma=False)
```

```python
import functools
import math

import jax
import jax.numpy as jnp
from jax import lax
from jax.experimental import pallas as pl
from jax.experimental.pallas import tpu as pltpu
from jax.sharding import PartitionSpec as P

MESH = pl.DeviceIdType.MESH
TWO_PI = 2.0 * math.pi
VMEM = pltpu.VMEM
NT = (((1,), (1,)), ((), ()))

SIN_COEFS = (4.442852586664358, -7.306899436200296, 3.59017447630795, -0.7735545907233887)
PHASE_STEPS = 34000.0


def half_turn_phasor(turns):
    r = turns - jnp.round(turns)
    u = r * r
    s = r * (SIN_COEFS[0] + u * (SIN_COEFS[1] + u * (SIN_COEFS[2] + u * SIN_COEFS[3])))
    q = s * s
    w = 2.000001 - q
    return 1.0 - q, s * (w * lax.rsqrt(w))


LAYERS = (1, 7, 4, 3, 5, 2, 6, 0)


def wrap(value, size):
    return jnp.where(value >= size, value - size, value)


def layer_at(i):
    layer = LAYERS[-1]
    for j, other in enumerate(LAYERS[:-1]):
        layer = jnp.where(i == j, other, layer)
    return layer


def whole_kernel(
    coords_hbm, positions_hbm, dest_hbm, directions_hbm, screen_hbm, freq_hbm, flux_hbm, index_hbm,
    out_hbm,
    strip, coords_ref, msg, got, addr_smem, wide, stage, sampled, back, blocks,
    positions_ref, dest_ref, directions_ref, freq_ref, flux_ref, index_ref,
    delays, turns, phase, phasor, intensity, inverse, total_ref,
    screen_sem, in_sem, addr_sem, ask_send, ask_recv, back_send, back_recv,
    z_send, z_recv, xy_send, xy_recv, vis_send, vis_recv, own_sem,
):
    g = lax.axis_index("stn")
    c = lax.axis_index("chan")
    n = 32
    z = g // 4
    sub = g % 4
    xh = sub // 2
    core = g % 2
    sibling = g + 1 - 2 * core
    rows = strip.shape[0]
    barrier = pltpu.get_barrier_semaphore()
    y = c // 2
    xl = c % 2
    chip = [(0, 1), (1, 0), (1, 1)]
    xy = [(0, h, l) for h, l in chip]
    xy += [(dy, h, l) for dy in (1, 3, 2) for h, l in [(0, 0)] + chip]
    stn = [(dz, r) for dz in LAYERS for r in range(4) if (dz, r) != (0, 0)]

    def xy_peer(dy, h, l):
        return (z * 4 + wrap(xh + h, 2) * 2 + core, wrap(y + dy, 4) * 2 + wrap(xl + l, 2))

    def stn_peer(dz, r):
        return wrap(z + dz, 8) * 4 + wrap(sub + r, 4)

    screen_copy = pltpu.make_async_copy(screen_hbm, strip, screen_sem)
    coords_copy = pltpu.make_async_copy(coords_hbm, coords_ref, in_sem.at[0])
    positions_copy = pltpu.make_async_copy(positions_hbm, positions_ref, in_sem.at[1])
    later = [
        pltpu.make_async_copy(source, target, in_sem.at[2 + i])
        for i, (source, target) in enumerate(
            (
                (dest_hbm, dest_ref),
                (directions_hbm, directions_ref),
                (freq_hbm, freq_ref),
                (flux_hbm, flux_ref),
                (index_hbm, index_ref),
            )
        )
    ]
    for copy in [coords_copy, positions_copy, screen_copy] + later:
        copy.start()
    for dz in (4, 3, 5, 2, 6, 1, 7, 0):
        for r in range(4):
            if dz or r:
                pl.semaphore_signal(
                    barrier, inc=1, device_id=(stn_peer(dz, r), c), device_id_type=MESH
                )
    for dy, h, l in xy:
        if dy or l:
            pl.semaphore_signal(barrier, inc=1, device_id=xy_peer(dy, h, l), device_id_type=MESH)
    positions_copy.wait()
    station_row = jnp.concatenate(
        [positions_ref[j : j + 1, :] for j in range(3)] + [jnp.zeros((1, 80), jnp.float32)], axis=1
    )
    msg[3] = jnp.broadcast_to((station_row * 2.0**24).astype(jnp.int32), (n, 128))
    coords_copy.wait()
    row_pos = coords_ref[0] * (rows - 1)
    col_pos = coords_ref[1] * (strip.shape[1] - 1)
    row_low = jnp.clip(jnp.floor(row_pos), 0.0, rows - 2.0)
    col_low = jnp.clip(jnp.floor(col_pos), 0.0, strip.shape[1] - 2.0)
    column = col_low.astype(jnp.int32)
    part = column // 127
    msg[0] = jnp.clip(part * rows + row_low.astype(jnp.int32), 0, 5 * rows - 2)
    msg[1] = ((row_pos - row_low) * 2.0**24).astype(jnp.int32)
    msg[2] = ((col_pos - (part * 127).astype(jnp.float32)) * 2.0**23).astype(jnp.int32)
    screen_copy.wait()
    step = 64

    def widen(i, carry):
        here = pl.ds(pl.multiple_of(i * step, step), step)
        lane = lax.broadcasted_iota(jnp.int32, (step, 128), 1)
        tiles = [strip[here, m * 128 : (m + 1) * 128] for m in range(4)]
        wide[here, :] = tiles[0]
        for b in range(1, 5):
            mixed = tiles[3] if b == 4 else jnp.where(lane >= 128 - b, tiles[b - 1], tiles[b])
            wide[pl.ds(pl.multiple_of(b * rows + i * step, step), step), :] = pltpu.roll(mixed, b, 1)
        return carry

    lax.fori_loop(0, rows // step, widen, 0)

    got[:, pl.ds(g, 1)] = msg[:, pl.ds(g, 1)]
    pl.semaphore_wait(barrier, n - 1 + 14)

    def ask(dz, r):
        to = wrap(z + 8 - dz, 8) * 4 + wrap(sub + r, 4)
        return pltpu.make_async_remote_copy(
            src_ref=msg.at[:, pl.ds(to, 1)],
            dst_ref=got.at[:, pl.ds(g, 1)],
            send_sem=ask_send.at[dz * 4 + r],
            recv_sem=ask_recv.at[dz * 4 + r],
            device_id=(to, c),
            device_id_type=MESH,
        )

    for dz, r in stn:
        ask(dz, r).start()
    for copy in later:
        copy.wait()

    def answer(dz, r):
        to = stn_peer(dz, r)
        return pltpu.make_async_remote_copy(
            src_ref=sampled.at[pl.ds(to, 1)],
            dst_ref=back.at[pl.ds(g, 1)],
            send_sem=back_send.at[dz * 4 + r],
            recv_sem=back_recv.at[dz * 4 + r],
            device_id=(to, c),
            device_id_type=MESH,
        )

    def cells_to_smem(dz):
        here = pl.ds(wrap(z + dz, 8) * 4, 4)
        return pltpu.make_async_copy(got.at[0, here], addr_smem.at[here], addr_sem.at[dz])

    def receive(dz):
        @pl.when(dz != 0)
        def _():
            ask(dz, 0).wait_recv()

        for r in range(1, 4):
            ask(dz, r).wait_recv()
        cells_to_smem(dz).start()

    depth = lax.broadcasted_iota(jnp.int32, (128, 128), 0).astype(jnp.float32)
    receive(LAYERS[0])

    def look_up(i, carry):
        dz = layer_at(i)

        @pl.when(i < 7)
        def _():
            receive(layer_at(i + 1))

        cells_to_smem(dz).wait()
        for r in range(4):
            to = stn_peer(dz, r)
            for j in range(128):
                stage[r, 2 * j : 2 * j + 2, :] = wide[pl.ds(addr_smem[to, j], 2), :]
            low = stage[r, pl.ds(0, 128, stride=2), :].T
            high = stage[r, pl.ds(1, 128, stride=2), :].T
            fy = got[1, pl.ds(to, 1), :].astype(jnp.float32) * 2.0**-24
            x = got[2, pl.ds(to, 1), :].astype(jnp.float32) * 2.0**-23
            mixed = (1.0 - fy) * low + fy * high
            tent = jnp.maximum(1.0 - jnp.abs(depth - x), 0.0)
            sampled[pl.ds(to, 1), :] = jnp.sum(mixed * tent, axis=0, keepdims=True)

        @pl.when(dz != 0)
        def _():
            answer(dz, 0).start()

        for r in range(1, 4):
            answer(dz, r).start()
        return carry

    lax.fori_loop(0, 8, look_up, 0)
    back[pl.ds(g, 1)] = sampled[pl.ds(g, 1)]
    for dz, r in stn:
        answer(dz, r).wait_recv()

    total = jnp.zeros((24, 128), jnp.float32)
    row_id = lax.broadcasted_iota(jnp.int32, (8, 128), 0)
    lane_id = lax.broadcasted_iota(jnp.int32, (128, 128), 0)
    for j in range(0, n, 2):
        left, right = [], []
        for o in (j, j + 1):
            v = back[o : o + 1, :]
            dest = dest_ref[o : o + 1, :]
            a = (dest // 64) % 8
            b = (dest // 512) * 64 + dest % 64
            hi = v.astype(jnp.bfloat16).astype(jnp.float32)
            mid = (v - hi).astype(jnp.bfloat16).astype(jnp.float32)
            lo = v - hi - mid
            hit = row_id == a
            left.append(
                jnp.concatenate([jnp.where(hit, part, 0.0) for part in (hi, mid, lo)], axis=0)
            )
            right.append(jnp.where(lane_id == b, 1.0, 0.0))
        total = total + lax.dot_general(
            jnp.concatenate(left, axis=1).astype(jnp.bfloat16),
            jnp.concatenate(right, axis=1).astype(jnp.bfloat16),
            NT,
            preferred_element_type=jnp.float32,
        )
    mine = jnp.round((total[0:8] + total[8:16] + total[16:24]) * (PHASE_STEPS / TWO_PI))
    mine = mine.astype(jnp.int32)
    own_rows = pl.ds(4 * z, 4)
    own_words = blocks.at[y, xh, xl, core, own_rows]
    own_words[...] = (mine[0:4] << 16) | (mine[4:8] & 0xFFFF)

    z_copies = []
    for k in (4, 3, 5, 2, 6, 1, 7, 0):
        for other in range(2):
            if k or other:
                copy = pltpu.make_async_remote_copy(
                    src_ref=own_words,
                    dst_ref=own_words,
                    send_sem=z_send.at[k * 2 + other],
                    recv_sem=z_recv.at[k * 2 + other],
                    device_id=(wrap(z + k, 8) * 4 + (sub + 1 - 2 * core if other else sub), c),
                    device_id_type=MESH,
                )
                copy.start()
                z_copies.append(copy)

    turned = (got[3].astype(jnp.float32) * 2.0**-24).T
    for block in range(n):
        cols = [turned[j * 16 : (j + 1) * 16, block : block + 1] for j in range(3)]
        for m in range(4):
            lanes = slice(m * 128, (m + 1) * 128)
            delays[m, block * 16 : (block + 1) * 16, :] = (
                cols[0] * directions_ref[0:1, lanes] + cols[1] * directions_ref[1:2, lanes]
            ) + cols[2] * directions_ref[2:3, lanes]
    half = freq_ref.shape[0] // 2
    sources = flux_ref.shape[0] * 128

    def prepare(i, carry):
        freq = freq_ref[core * half + i]
        turns[i] = freq * delays[...]
        freq = jnp.full((8, 128), freq, jnp.float32)
        inverse[i] = (1.0 / PHASE_STEPS) / freq
        intensity[i] = (
            flux_ref[...]
            * jnp.exp(index_ref[...] * jnp.log(freq[0:4]))
            * (1.0 / math.sqrt(sources))
        )
        total_ref[i] = jnp.zeros(total_ref.shape[1:], jnp.float32)
        return carry

    lax.fori_loop(0, half // 2, prepare, 0)

    for copy in z_copies:
        copy.wait_recv()

    def pass_on(dy, h, l):
        block = blocks.at[y, xh, xl]
        return pltpu.make_async_remote_copy(
            src_ref=block,
            dst_ref=block,
            send_sem=xy_send.at[dy * 4 + h * 2 + l],
            recv_sem=xy_recv.at[dy * 4 + h * 2 + l],
            device_id=xy_peer(dy, h, l),
            device_id_type=MESH,
        )

    for dy, h, l in xy:
        pass_on(dy, h, l).start()
    lax.fori_loop(half // 2, half, prepare, 0)

    lane = lax.broadcasted_iota(jnp.int32, (8, 128), 1)
    sublane = lax.broadcasted_iota(jnp.int32, (8, 128), 0)

    def spread(k):
        @pl.when(k > 0)
        def _():
            pass_on(k, 0, 0).wait_recv()

        for h, l in chip:
            pass_on(k, h, l).wait_recv()
        m = wrap(y + 4 - k, 4)
        for pair in range(4):
            here = slice(pair * 8, (pair + 1) * 8)
            for group in range(4):
                kk, hh = group % 2, group // 2
                high, low = [], []
                for words in (blocks[m, hh, 0, kk, here], blocks[m, hh, 1, kk, here]):
                    high.append((words >> 16).astype(jnp.float32))
                    low.append(((words << 16) >> 16).astype(jnp.float32))
                for which in range(2):
                    even, odd = [
                        jnp.where(sublane < 4, hi, pltpu.roll(lo, 4, 0))
                        if which == 0
                        else jnp.where(sublane < 4, pltpu.roll(hi, 4, 0), lo)
                        for hi, lo in zip(high, low)
                    ]
                    first = ((2 * pair + which) * 4 + group) * 16
                    phase[first : first + 8] = jnp.where(lane < 64, even, pltpu.roll(odd, 64, 1))
                    phase[first + 8 : first + 16] = jnp.where(
                        lane < 64, pltpu.roll(even, 64, 1), odd
                    )

    stations = phase.shape[0]
    tile = 16
    chip_rows = pl.ds(pl.multiple_of((g // 2) * 32, 32), 32)

    def add_channels(k, first, count):
        m = wrap(y + 4 - k, 4)
        for j in range(count):
            f = first + j
            inv = inverse[f, 0:1]

            def phasors(here):
                re, im = half_turn_phasor(turns[f, m, here, :] + inv * phase[here, :])
                return re.astype(jnp.bfloat16), im.astype(jnp.bfloat16)

            re, im = phasors(chip_rows)
            weight = intensity[f, pl.ds(m, 1)]
            re = (re.astype(jnp.float32) * weight).astype(jnp.bfloat16)
            im = (im.astype(jnp.float32) * weight).astype(jnp.bfloat16)
            left = jnp.concatenate(
                [jnp.concatenate([re, im], axis=1), jnp.concatenate([im, -re], axis=1)], axis=0
            )
            for t in range(stations // tile):
                here = slice(t * tile, (t + 1) * tile)
                re, im = phasors(here)
                phasor[j, here, :128] = re
                phasor[j, here, 128:] = im
            result = lax.dot_general(left, phasor[j], NT, preferred_element_type=jnp.float32)
            total_ref[f] = total_ref[f] + result.reshape(total_ref.shape[1:])

    def send(i, count):
        here = pl.ds(i * count, count)
        there = pl.ds(core * half + i * count, count)
        return (
            pltpu.make_async_copy(total_ref.at[here, :, core], out_hbm.at[there], own_sem.at[i]),
            pltpu.make_async_remote_copy(
                src_ref=total_ref.at[here, :, 1 - core],
                dst_ref=out_hbm.at[there],
                send_sem=vis_send.at[i],
                recv_sem=vis_recv.at[i],
                device_id=(sibling, c),
                device_id_type=MESH,
            ),
        )

    def finish(i, count):
        lanes = pl.ds(pl.multiple_of((g // 8) * 128, 128), 128)
        row = lax.broadcasted_iota(jnp.int32, (2, 16, 128), 0) * 16
        row = row + lax.broadcasted_iota(jnp.int32, (2, 16, 128), 1) + ((g // 2) % 4) * 32
        cross = lax.broadcasted_iota(jnp.int32, (2, 16, 128), 2) != row
        for j in range(count):
            for part in range(2):
                block = total_ref[i * count + j, part, :, :, lanes]
                total_ref[i * count + j, part, :, :, lanes] = jnp.where(cross, block, 0.0)
        for copy in send(i, count):
            copy.start()

    quarter = half // 4

    def chunk(k, carry):
        dy = jnp.where(k == 2, 3, k)
        spread(dy)
        add_channels(dy, 0, half)
        return carry

    lax.fori_loop(0, 3, chunk, 0)
    spread(2)

    def last(i, carry):
        add_channels(2, i * quarter, quarter)
        finish(i, quarter)
        return carry

    lax.fori_loop(0, 4, last, 0)
    for dz, r in stn:
        ask(dz, r).wait_send()
        answer(dz, r).wait_send()
    for copy in z_copies:
        copy.wait_send()
    for dy, h, l in xy:
        pass_on(dy, h, l).wait_send()
    for k in range(4):
        for copy in send(k, quarter):
            copy.wait()


def whole(coords, positions, dest, directions, strip, freq, flux, index):
    dma = pltpu.SemaphoreType.DMA
    n = dest.shape[0]
    rows = strip.shape[0]
    channels = freq.shape[0]
    half = channels // 2
    stations = 16 * n
    bf16, f32 = jnp.bfloat16, jnp.float32
    return pl.pallas_call(
        whole_kernel,
        out_shape=jax.ShapeDtypeStruct((channels, 2, 16, stations), f32),
        in_specs=[pl.BlockSpec(memory_space=pl.ANY)] * 8,
        out_specs=pl.BlockSpec(memory_space=pl.ANY),
        scratch_shapes=[
            VMEM(strip.shape, f32),
            VMEM((2, n, 128), f32),
            VMEM((4, n, 128), jnp.int32),
            VMEM((4, n, 128), jnp.int32),
            pltpu.SMEM((n, 128), jnp.int32),
            VMEM((5 * rows, 128), f32),
            VMEM((4, 256, 128), f32),
            VMEM((n, 128), f32),
            VMEM((n, 128), f32),
            VMEM((4, 2, 2, 2, 32, 128), jnp.int32),
            VMEM(positions.shape, f32),
            VMEM(dest.shape, jnp.int32),
            VMEM(directions.shape, f32),
            pltpu.SMEM(freq.shape, f32),
            VMEM(flux.shape, f32),
            VMEM(index.shape, f32),
            VMEM((4, stations, 128), f32),
            VMEM((half, 4, stations, 128), f32),
            VMEM((stations, 128), f32),
            VMEM((half, stations, 256), bf16),
            VMEM((half, 4, 128), f32),
            VMEM((half, 8, 128), f32),
            VMEM((half, 2, 2, 16, stations), f32),
            dma, dma((8,)), dma((8,)),
            dma((32,)), dma((32,)),
            dma((32,)), dma((32,)),
            dma((16,)), dma((16,)),
            dma((16,)), dma((16,)),
            dma((4,)), dma((4,)), dma((4,)),
        ],
        compiler_params=pltpu.CompilerParams(
            collective_id=1, has_side_effects=True, vmem_limit_bytes=60 << 20
        ),
        name="whole",
    )(coords, positions, dest, directions, strip, freq, flux, index)


def hand_on_kernel(in_hbm, out_hbm, held, in_sem, out_sem):
    parts = in_sem.shape[0]
    size = in_hbm.shape[0] // parts
    slices = [slice(i * size, (i + 1) * size) for i in range(parts)]
    loads = [
        pltpu.make_async_copy(in_hbm.at[here], held.at[here], in_sem.at[i])
        for i, here in enumerate(slices)
    ]
    stores = [
        pltpu.make_async_copy(held.at[here], out_hbm.at[here], out_sem.at[i])
        for i, here in enumerate(slices)
    ]
    for load in loads:
        load.start()
    for load, store in zip(loads, stores):
        load.wait()
        store.start()
    for store in stores:
        store.wait()


def hand_on(x):
    return pl.pallas_call(
        hand_on_kernel,
        out_shape=jax.ShapeDtypeStruct(x.shape, x.dtype),
        in_specs=[pl.BlockSpec(memory_space=pl.ANY)],
        out_specs=pl.BlockSpec(memory_space=pl.ANY),
        scratch_shapes=[
            VMEM(x.shape, x.dtype),
            pltpu.SemaphoreType.DMA((4,)),
            pltpu.SemaphoreType.DMA((4,)),
        ],
        compiler_params=pltpu.CompilerParams(vmem_limit_bytes=60 << 20),
        name="hand_on",
    )(x)


def body(
    screen, pierce_coords, query_dest, positions, directions, freq_ratio, source_flux, spectral_index
):
    groups = lax.axis_size("stn")
    capacity = query_dest.shape[3]
    rows = screen.shape[0] * screen.shape[1]
    cols = screen.shape[2]
    coords = pierce_coords.reshape(2, groups, capacity)
    visible = whole(
        coords,
        positions,
        query_dest.reshape(groups, capacity),
        directions,
        screen.reshape(rows, cols),
        freq_ratio,
        source_flux.reshape(-1, 128),
        spectral_index.reshape(-1, 128),
    )
    return hand_on(visible)


def solution(mesh):
    in_specs = (
        P("stn", None, None),
        P(None, "stn", "chan", None, None),
        P("stn", "chan", None, None),
        P(None, "stn"),
        P(),
        P("chan"),
        P(),
        P(),
    )
    out_specs = P("chan", None, "stn", None)
    return jax.shard_map(body, mesh=mesh, in_specs=in_specs, out_specs=out_specs, check_vma=False)
```
